512 devices in a mesh: gx: 16 (over x_lo, z), gy: 32 (over y, x_hi, core).
Axes of the slice: x: 4 (x_hi: 2, x_lo: 2; x = x_hi * 2 + x_lo), y: 8, z: 8, core: 2. Of those that a mesh axis runs over, the one named last changes fastest.
Arguments:
- fields: float32 [5, 16, 256, 4096], P(None, None, 'gx', 'gy'), may hold values from -6 to 6
- diffusivity: float32 [16, 256, 4096], P(None, 'gx', 'gy'), may hold values from 0.03 to 0.3
- heights: int32 [256, 4096], P('gx', 'gy'), may hold values from 0 to 8
- wrap_map: int32 [4096], replicated, may hold values from 0 to 4095, each once
Outputs:
- advanced: float32 [5, 16, 256, 4096], P(None, None, 'gx', 'gy')
The draws below stay inside these ranges and needn't reach their ends.
Inputs may be any that keep to these rules, and one draw needn't show every extreme that they name: `wrap_map`: each spanwise column appears exactly once.
All inputs are finite; a program needn't handle non-finite values.
Results may differ from the reference program's by a relative error of at most 0.00002.
Values sent between devices are 32-bit elements; how exact they have to be, the bound alone decides.
No kernel may reach another device: no remote copies, remote signals or barrier semaphores. Data moves between devices by JAX's collectives and lax.ppermute only.
A program may use at most 64 MiB of HBM per device.

```python
import math
import jax
import jax.numpy as jnp
from jax import lax

NZ = 16
NX = 256
NY = 4096


def touch_ends(entries, rng, smallest, top_value):
    place = [jax.random.randint(jax.random.fold_in(rng, axis), (), 0, length) for axis, length in enumerate(entries.shape)]
    longest = entries.shape.index(max(entries.shape))
    beside = place[:longest] + [(place[longest] + 1) % entries.shape[longest]] + place[longest + 1:]
    return entries.at[tuple(place)].set(smallest).at[tuple(beside)].set(top_value)


def steps_of(stream_key, shape, pieces, smallest, high):
    def one(axis_at, parts):
        steps = jax.random.uniform(jax.random.fold_in(jax.random.fold_in(stream_key, 6), axis_at), (parts,), jnp.float32, smallest / len(pieces), high / len(pieces))
        return jnp.repeat(jnp.exp(steps), shape[axis_at] // parts).reshape((-1,) + (1,) * (len(shape) - axis_at - 1))

    loudness = one(*pieces[0])
    for cut in pieces[1:]:
        loudness = loudness * one(*cut)
    return loudness


def noise(rng, shape, spread, most, pieces=(), held_as=jnp.bfloat16):
    drawn = jax.random.normal(rng, shape, jnp.float32) * spread
    if len(pieces) > 0:
        drawn = steps_of(rng, shape, pieces, -0.22, 0.18) * drawn
    return jnp.clip(drawn, min=-most, max=most).astype(held_as)


def setup_inputs(seed: int = 0) -> dict:
    splits = jax.random.split(jax.random.key(seed), 5)
    return {
        "fields": noise(splits[0], (5, NZ, NX, NY), 1.0, 6.0, ((2, 16), (3, 32)), jnp.float32),
        "diffusivity": jnp.clip(jnp.exp(math.log(0.3) - 2.3025852 * jax.random.uniform(splits[1], (NZ, NX, NY), jnp.float32) ** steps_of(splits[1], (NZ, NX, NY), ((1, 16), (2, 32)), -0.2, 0.2)), 0.03, 0.3),
        "heights": touch_ends(jax.random.randint(splits[2], (NX, NY), 0, NZ // 2 + 1), jax.random.fold_in(splits[2], 1), 0, (NZ // 2 + 1) - 1).astype(jnp.int32),
        "wrap_map": jax.random.permutation(splits[3], NY).astype(jnp.int32),
    }


DRAG_COEF = 1.0
TIME_STEP = 0.3
BUOYANCY = 0.5
SPEED_EPS = 0.01

def transport(extended, wind_parts, diff_ext):
    centre = extended[:, 1:-1, 1:-1]
    east_cell = extended[:, 2:, 1:-1]
    west_cell = extended[:, :-2, 1:-1]
    north_cell = extended[:, 1:-1, 2:]
    south_cell = extended[:, 1:-1, :-2]
    padded = jnp.pad(centre, ((1, 1), (0, 0), (0, 0)))
    upper_cell = padded[2:]
    lower_cell = padded[:-2]
    advect = 0.5 * (wind_parts[0] * (east_cell - west_cell) + wind_parts[1] * (north_cell - south_cell) + wind_parts[2] * (upper_cell - lower_cell))
    diff_mid = diff_ext[:, 1:-1, 1:-1]
    diff_pad = jnp.pad(diff_mid, ((1, 1), (0, 0), (0, 0)), mode='edge')
    diffuse = 0.5 * ((diff_mid + diff_ext[:, 2:, 1:-1]) * (east_cell - centre) + (diff_mid + diff_ext[:, :-2, 1:-1]) * (west_cell - centre) + (diff_mid + diff_ext[:, 1:-1, 2:]) * (north_cell - centre) + (diff_mid + diff_ext[:, 1:-1, :-2]) * (south_cell - centre) + (diff_mid + diff_pad[2:]) * (upper_cell - centre) + (diff_mid + diff_pad[:-2]) * (lower_cell - centre))
    return diffuse - advect

def tendency(extended, diff_ext, drag_ext, mapper):
    centre = extended[:, :, 1:-1, 1:-1]
    wind_parts = centre[:3]
    rates = mapper(lambda column: transport(column, wind_parts, diff_ext), extended)
    wind_speed = jnp.sqrt(centre[0] * centre[0] + centre[1] * centre[1] + centre[2] * centre[2] + SPEED_EPS)
    resist = drag_ext[:, 1:-1, 1:-1] * wind_speed
    vertical = rates[2] - resist * centre[2] + BUOYANCY * centre[3]
    return jnp.concatenate([rates[:2] - resist * centre[:2], vertical[None], rates[3:]], 0)

def wrap_pad(values, forward, backward, rim_width):
    lower_rim = jnp.take(values[..., -rim_width:, :], backward, axis=-1)
    upper_rim = jnp.take(values[..., :rim_width, :], forward, axis=-1)
    extended = jnp.concatenate([lower_rim, values, upper_rim], -2)
    return jnp.concatenate([extended[..., -rim_width:], extended, extended[..., :rim_width]], -1)

def reference(fields, diffusivity, heights, wrap_map):
    forward = wrap_map.astype(jnp.int32)
    columns = jnp.arange(forward.shape[0], dtype=jnp.int32)
    backward = jnp.zeros_like(forward).at[forward].set(columns)
    levels = lax.broadcasted_iota(jnp.int32, diffusivity.shape, 0)
    drag_coef = jnp.where(levels < heights[None], DRAG_COEF, 0.0).astype(diffusivity.dtype)
    diff_ext = wrap_pad(diffusivity, forward, backward, 1)
    drag_ext = wrap_pad(drag_coef, forward, backward, 1)

    def rate(values):
        return tendency(wrap_pad(values, forward, backward, 1), diff_ext, drag_ext, lax.map)
    section_one = fields + TIME_STEP / 3.0 * rate(fields)
    return fields + TIME_STEP / 2.0 * rate(section_one)
```

```python
import functools

import jax
import jax.numpy as jnp
from jax import lax
from jax.experimental import pallas as pl
from jax.experimental.pallas import tpu as pltpu
from jax.sharding import PartitionSpec as P

DRAG_COEF = 1.0
TIME_STEP = 0.3
BUOYANCY = 0.5
SPEED_EPS = 0.01

NF = 5
NA = 6
NZ = 16
NI = 16
NJ = 128
RIM = NA * NZ
EDGE_ROWS = 2 * RIM + 8
BLOCK = NA * NZ * NI
PACK = BLOCK + 2 * RIM + 64
HEIGHT_AT = BLOCK + 2 * RIM

VMEM = pl.BlockSpec(memory_space=pltpu.VMEM)
EXACT = lax.Precision.HIGHEST


def iota(shape, dim):
    return lax.broadcasted_iota(jnp.int32, shape, dim)


def call(kernel, outs, *args, scratch=(), name=None):
    return pl.pallas_call(
        kernel,
        out_shape=outs,
        in_specs=[VMEM] * len(args),
        out_specs=jax.tree.map(lambda _: VMEM, outs),
        scratch_shapes=list(scratch),
        compiler_params=pltpu.CompilerParams(vmem_limit_bytes=40 * 1024 * 1024),
        name=name,
    )(*args)


def f32(*shape):
    return jax.ShapeDtypeStruct(shape, jnp.float32)


def edges_kernel(fields, diff, heights, east, west):
    for out, near, far in ((east, NI - 1, NI - 2), (west, 0, 1)):
        for a in range(NA):
            src = diff if a == NF else fields.at[a]
            out[a * NZ:(a + 1) * NZ, :] = src[:, near, :]
            out[RIM + a * NZ:RIM + (a + 1) * NZ, :] = src[:, far, :]
        row = heights[near:near + 1, :].astype(jnp.float32)
        out[2 * RIM:EDGE_ROWS, :] = jnp.broadcast_to(row, (8, NJ))


def picks():
    row, lane = iota((8, NJ), 0), iota((8, NJ), 1)
    want = jnp.where(row < 2, row, jnp.where(row < 4, NJ - 4 + row, -1))
    return jnp.where(lane == want, 1.0, 0.0).astype(jnp.float32)


def pack_kernel(fields, diff, heights, west, east, to_a, to_b):
    even = lax.rem(lax.axis_index("gy"), 2) == 0
    rows = jnp.concatenate(
        [
            fields[...].reshape(NF * NZ * NI, NJ),
            diff[...].reshape(NZ * NI, NJ),
            west[0:RIM, :],
            east[0:RIM, :],
            heights[...].astype(jnp.float32),
            jnp.zeros((PACK - HEIGHT_AT - NI, NJ), jnp.float32),
        ],
        0,
    )
    cols = lax.dot_general(
        picks(), rows, (((1,), (1,)), ((), ())), precision=EXACT, preferred_element_type=jnp.float32
    )
    low, high = cols[0:2, :], cols[2:4, :]
    to_a[...] = jnp.where(even, high, low)
    to_b[...] = jnp.where(even, low, high)


def levels(x, edge):
    k = iota(x.shape, 0)
    above = jnp.where(k == NZ - 1, x if edge else 0.0, pltpu.roll(x, NZ - 1, 0))
    below = jnp.where(k == 0, x if edge else 0.0, pltpu.roll(x, 1, 0))
    return above, below


def row_rates(near, far, height, sign):
    u, v, w = near[0], near[1], near[2]
    k_cell = near[NF]
    k_above, k_below = levels(k_cell, True)
    drag = jnp.where(iota(u.shape, 0).astype(jnp.float32) < height, DRAG_COEF, 0.0)
    resist = drag * jnp.sqrt(u * u + v * v + w * w + SPEED_EPS)
    rates = []
    for m in range(NF):
        f = near[m]
        above, below = levels(f, False)
        rate = 0.5 * (
            (k_cell + far[NF]) * (far[m] - f)
            + (k_cell + k_above) * (above - f)
            + (k_cell + k_below) * (below - f)
            + sign * u * far[m]
            - w * (above - below)
        )
        if m < 3:
            rate = rate - resist * f
        if m == 2:
            rate = rate + BUOYANCY * near[3]
        rates.append(rate)
    return rates


def split_rim(rim):
    near = [rim[a * NZ:(a + 1) * NZ, :] for a in range(NA)]
    far = [rim[RIM + a * NZ:RIM + (a + 1) * NZ, :] for a in range(NA)]
    return near, far, rim[2 * RIM:2 * RIM + 1, :]


def packet_kernel(west, east, out):
    first = lax.axis_index("gx") == 0
    rim = jnp.where(first, west[...], east[...])
    sign = jnp.where(first, 1.0, -1.0).astype(jnp.float32)
    near, far, height = split_rim(rim)
    rates = row_rates(near, far, height, sign)
    zero = jnp.zeros((NZ, NJ), jnp.float32)
    lower = [near[0], near[1], near[2], near[NF], rates[0], rates[1], rates[2], zero]
    upper = [near[3], near[4], near[1], near[NF], rates[3], rates[4], zero, zero]
    for row in range(8):
        out[0:NZ, row, :] = lower[row]
        out[NZ:2 * NZ, row, :] = upper[row]


def inverse_kernel(wrap, out):
    total = jnp.zeros((64, NJ), jnp.float32)
    lane = iota((32, NJ), 1).astype(jnp.float32)
    for s in range(32):
        p = wrap[s:s + 1, :]
        hit = jnp.where(iota((32, NJ), 0) == p // NJ, 1.0, 0.0)
        low = jnp.where(iota((NJ, NJ), 0) == lax.rem(p, NJ), 1.0, 0.0).astype(jnp.bfloat16)
        left = jnp.concatenate([hit * lane, hit * float(s)], 0).astype(jnp.bfloat16)
        total = total + lax.dot_general(
            left, low, (((1,), (1,)), ((), ())), preferred_element_type=jnp.float32
        )
    out[...] = (total[0:32, :] + NJ * total[32:64, :]).astype(jnp.int32)


def permute_kernel(rows, wrap, inverse, out, index, held):
    first = lax.axis_index("gx") == 0
    index[...] = jnp.where(first, inverse[...], wrap[...])
    upper = lax.axis_index("gy") >= NZ
    x = rows[...]
    lane, sub = iota(x.shape, 2), iota(x.shape, 1)

    def after(y):
        return jnp.concatenate([y[1:], y[:1]], 0)

    def before(y):
        return jnp.concatenate([y[-1:], y[:-1]], 0)

    left, right = pltpu.roll(x, NJ - 1, 2), pltpu.roll(x, 1, 2)
    north = jnp.where(lane == NJ - 1, after(left), left)
    south = jnp.where(lane == 0, before(right), right)
    v = jnp.where(upper, x[:, 2:3, :], x[:, 1:2, :])
    k_cell, k_north, k_south = x[:, 3:4, :], north[:, 3:4, :], south[:, 3:4, :]
    term = 0.5 * (
        (k_cell + k_north) * (north - x) + (k_cell + k_south) * (south - x) - v * (north - south)
    )
    held[...] = x + jnp.where((sub >= 4) & (sub < 7), pltpu.roll(term, 4, 1), 0.0)

    def target(t, _):
        idx = jnp.broadcast_to(index[pl.ds(t, 1), :], (8, NJ))
        hi, lo = lax.shift_right_logical(idx, 7), lax.bitwise_and(idx, NJ - 1)
        acc = jnp.zeros((8, NJ), jnp.float32)
        for s in range(32):
            got = jnp.take_along_axis(held[s], lo, axis=1, mode="promise_in_bounds")
            acc = jnp.where(hi == s, got, acc)
        out[t] = acc
        return 0

    lax.fori_loop(0, 32, target, 0)
    y = out[...]
    prior, later = before(y), after(y)
    last = jnp.zeros_like(y)
    for r in range(4):
        corner = jnp.where(lane < 64, pltpu.roll(later, r, 2), pltpu.roll(prior, (NJ - r) % NJ, 2))
        corner = pltpu.roll(corner, 7 - r, 1)
        last = jnp.where((lane == r) | (lane == NJ - 1 - r), corner, last)
    out[...] = jnp.where(sub == 7, last, y)


def final_kernel(
    fields, diff, heights, west, east, from_a, from_b, wrapped, out,
    halo, one, one_halo, rim_w, rim_e, corner_w, corner_e, one_w, one_e,
):
    gx = lax.axis_index("gx")
    first, final = gx == 0, gx == lax.axis_size("gx") - 1
    even = lax.rem(lax.axis_index("gy"), 2) == 0
    a, b = from_a[...], from_b[...]
    north, south = jnp.where(even, a, b), jnp.where(even, b, a)
    cols = jnp.concatenate([north, south, jnp.zeros((4, PACK), jnp.float32)], 0)
    halo[...] = lax.dot_general(
        cols, picks(), (((0,), (0,)), ((), ())), precision=EXACT, preferred_element_type=jnp.float32
    )

    lane, sub = iota((NI, NJ), 1), iota((NI, NJ), 0)
    place = {0: (0, 0), 1: (0, 1), 2: (0, 2), NF: (0, 3), 3: (NZ, 0), 4: (NZ, 1)}

    def beside(m, h):
        m_left, h_left = pltpu.roll(m, NJ - 1, 1), pltpu.roll(h, NJ - 1, 1)
        m_right, h_right = pltpu.roll(m, 1, 1), pltpu.roll(h, 1, 1)
        at_end, at_start = lane == NJ - 1, lane == 0
        return (
            jnp.where(at_end, h_left, m_left),
            jnp.where(at_start, h_right, m_right),
            jnp.where(at_end, m_left, h_left),
            jnp.where(at_start, m_right, h_right),
        )

    for rim, mine, sign, own_row, rim_out, corner_at, corner_out, one_out in (
        (west, first, 1.0, 0, rim_w, BLOCK, corner_w, one_w),
        (east, final, -1.0, NI - 1, rim_e, BLOCK + RIM, corner_e, one_e),
    ):
        near, far, height = split_rim(rim[...])
        rates = row_rates(near, far, height, sign)
        corners = [halo[corner_at + i * NZ:corner_at + (i + 1) * NZ, :] for i in range(NA)]
        sides = [beside(near[i], corners[i]) for i in range(NA)]
        k_cell, k_n, k_s = near[NF], sides[NF][0], sides[NF][1]
        for m in range(NF):
            f, n, s = near[m], sides[m][0], sides[m][1]
            rates[m] = rates[m] + 0.5 * (
                (k_cell + k_n) * (n - f) + (k_cell + k_s) * (s - f) - near[1] * (n - s)
            )
            half, row = (0, 4 + m) if m < 3 else (NZ, 1 + m)
            rates[m] = jnp.where(mine, wrapped[half:half + NZ, row, :], rates[m])
        for i in range(NA):
            half, row = place[i]
            near[i] = jnp.where(mine, wrapped[half:half + NZ, row, :], near[i])
            spare = wrapped[half:half + NZ, 7, :]
            spare = jnp.where(lane < 64, pltpu.roll(spare, (NJ - row) % NJ, 1), pltpu.roll(spare, row, 1))
            rim_out[i * NZ:(i + 1) * NZ, :] = near[i]
            corner_out[i * NZ:(i + 1) * NZ, :] = jnp.where(mine, spare, corners[i])
        k_own = diff[:, own_row, :]
        for m in range(NF):
            own = fields[m, :, own_row, :]
            rate = rates[m] + 0.5 * ((near[NF] + k_own) * (own - near[m]) - sign * near[0] * own)
            one_out[m * NZ:(m + 1) * NZ, :] = near[m] + TIME_STEP / 3.0 * rate

    def row_of(ref, i, k):
        return ref[pl.ds(i * NZ + k, 1), :]

    def along(x, low, high):
        return (
            jnp.where(sub == NI - 1, high, pltpu.roll(x, NI - 1, 0)),
            jnp.where(sub == 0, low, pltpu.roll(x, 1, 0)),
        )

    def halo_tile(i, k):
        at = pl.multiple_of((i * NZ + k) * NI, NI)
        return halo[pl.ds(at, NI), :]

    def rates_of(cells, k_cell, k_sides, drag):
        u, v, w = cells[0][0], cells[1][0], cells[2][0]
        resist = drag * jnp.sqrt(u * u + v * v + w * w + SPEED_EPS)
        sums = [k_cell + side for side in k_sides]
        total = sums[0] + sums[1] + sums[2] + sums[3] + sums[4] + sums[5]
        rates = []
        for m in range(NF):
            f, e, ws, n, s, up, dn = cells[m]
            rate = 0.5 * (
                (sums[0] - u) * e + (sums[1] + u) * ws
                + (sums[2] - v) * n + (sums[3] + v) * s
                + (sums[4] - w) * up + (sums[5] + w) * dn
                - total * f
            )
            if m < 3:
                rate = rate - resist * f
            if m == 2:
                rate = rate + BUOYANCY * cells[3][0]
            rates.append(rate)
        return rates

    high_main = heights[...].astype(jnp.float32)
    high_halo = halo[HEIGHT_AT:HEIGHT_AT + NI, :]

    def section_one(k, _):
        up, dn = jnp.minimum(k + 1, NZ - 1), jnp.maximum(k - 1, 0)
        has_up = jnp.where(k < NZ - 1, 1.0, 0.0).astype(jnp.float32)
        has_dn = jnp.where(k > 0, 1.0, 0.0).astype(jnp.float32)
        level = k.astype(jnp.float32)
        k_main, k_halo = diff[k], halo_tile(NF, k)
        n, s, hn, hs = beside(k_main, k_halo)
        e, ws = along(k_main, row_of(rim_w, NF, k), row_of(rim_e, NF, k))
        he, hw = along(k_halo, row_of(corner_w, NF, k), row_of(corner_e, NF, k))
        k_sides = (e, ws, n, s, diff[up], diff[dn])
        kh_sides = (he, hw, hn, hs, halo_tile(NF, up), halo_tile(NF, dn))
        cells, halos = [], []
        for m in range(NF):
            f, h = fields[m, k], halo_tile(m, k)
            n, s, hn, hs = beside(f, h)
            e, ws = along(f, row_of(rim_w, m, k), row_of(rim_e, m, k))
            he, hw = along(h, row_of(corner_w, m, k), row_of(corner_e, m, k))
            cells.append((f, e, ws, n, s, has_up * fields[m, up], has_dn * fields[m, dn]))
            halos.append((h, he, hw, hn, hs, has_up * halo_tile(m, up), has_dn * halo_tile(m, dn)))
        drag = jnp.where(level < high_main, DRAG_COEF, 0.0)
        drag_h = jnp.where(level < high_halo, DRAG_COEF, 0.0)
        rates = rates_of(cells, k_main, k_sides, drag)
        rates_h = rates_of(halos, k_halo, kh_sides, drag_h)
        for m in range(NF):
            one[m, k] = cells[m][0] + TIME_STEP / 3.0 * rates[m]
            one_halo[m, k] = halos[m][0] + TIME_STEP / 3.0 * rates_h[m]
        return 0

    lax.fori_loop(0, NZ, section_one, 0)

    def section_two(k, _):
        up, dn = jnp.minimum(k + 1, NZ - 1), jnp.maximum(k - 1, 0)
        has_up = jnp.where(k < NZ - 1, 1.0, 0.0).astype(jnp.float32)
        has_dn = jnp.where(k > 0, 1.0, 0.0).astype(jnp.float32)
        k_main = diff[k]
        n, s, _, _ = beside(k_main, halo_tile(NF, k))
        e, ws = along(k_main, row_of(rim_w, NF, k), row_of(rim_e, NF, k))
        k_sides = (e, ws, n, s, diff[up], diff[dn])
        cells = []
        for m in range(NF):
            f = one[m, k]
            n, s, _, _ = beside(f, one_halo[m, k])
            e, ws = along(f, row_of(one_w, m, k), row_of(one_e, m, k))
            cells.append((f, e, ws, n, s, has_up * one[m, up], has_dn * one[m, dn]))
        drag = jnp.where(k.astype(jnp.float32) < high_main, DRAG_COEF, 0.0)
        rates = rates_of(cells, k_main, k_sides, drag)
        for m in range(NF):
            out[m, k] = fields[m, k] + TIME_STEP / 2.0 * rates[m]
        return 0

    lax.fori_loop(0, NZ, section_two, 0)


def shards(fields, diffusivity, heights, wrap_map):
    count_x, count_y = lax.axis_size("gx"), lax.axis_size("gy")
    edge = f32(EDGE_ROWS, NJ)
    to_east, to_west = call(edges_kernel, (edge, edge), fields, diffusivity, heights, name="edges")
    east_pairs = [(i, (i + 1) % count_x) for i in range(count_x)]
    west = lax.ppermute(to_east, "gx", east_pairs)
    east = lax.ppermute(to_west, "gx", [(j, i) for i, j in east_pairs])

    wrap = wrap_map.reshape(count_y, NJ)
    inverse = call(
        inverse_kernel, jax.ShapeDtypeStruct((count_y, NJ), jnp.int32), wrap, name="inverse"
    )

    packets = call(packet_kernel, f32(count_y, 8, NJ), west, east, name="packets")
    pack = f32(2, PACK)
    to_a, to_b = call(pack_kernel, (pack, pack), fields, diffusivity, heights, west, east, name="pack")
    low_pairs = [(i, i + 1) for i in range(0, count_y, 2)]
    high_pairs = [(i, (i + 1) % count_y) for i in range(1, count_y, 2)]
    from_a = lax.ppermute(to_a, "gy", low_pairs + [(j, i) for i, j in low_pairs])
    from_b = lax.ppermute(to_b, "gy", high_pairs + [(j, i) for i, j in high_pairs])

    rows = lax.all_to_all(packets, "gy", 0, 0)
    moved = call(
        permute_kernel, f32(count_y, 8, NJ), rows, wrap, inverse, name="permute",
        scratch=[pltpu.VMEM((32, NJ), jnp.int32), pltpu.VMEM((32, 8, NJ), jnp.float32)],
    )
    wrapped = lax.all_to_all(moved, "gy", 0, 0)

    state = pltpu.VMEM((NF, NZ, NI, NJ), jnp.float32)
    rim = pltpu.VMEM((RIM, NJ), jnp.float32)
    return call(
        final_kernel, f32(NF, NZ, NI, NJ),
        fields, diffusivity, heights, west, east, from_a, from_b, wrapped, name="sections",
        scratch=[pltpu.VMEM((PACK, NJ), jnp.float32), state, state, rim, rim, rim, rim, rim, rim],
    )


def solution(mesh):
    in_specs = (P(None, None, "gx", "gy"), P(None, "gx", "gy"), P("gx", "gy"), P())
    out_specs = P(None, None, "gx", "gy")
    return jax.shard_map(shards, mesh=mesh, in_specs=in_specs, out_specs=out_specs, check_vma=False)
```

```python
import functools

import jax
import jax.numpy as jnp
from jax import lax
from jax.experimental import pallas as pl
from jax.experimental.pallas import tpu as pltpu
from jax.sharding import PartitionSpec as P

DRAG_COEF = 1.0
TIME_STEP = 0.3
BUOYANCY = 0.5
SPEED_EPS = 0.01

NF = 5
NA = 6
NZ = 16
NI = 16
NJ = 128
RIM = NA * NZ
EDGE_ROWS = 2 * RIM + 8
MESSAGE = EDGE_ROWS + 8
BLOCK = NA * NZ * NI
PACK = BLOCK + 128
HEIGHT_AT = BLOCK

VMEM = pl.BlockSpec(memory_space=pltpu.VMEM)
EXACT = lax.Precision.HIGHEST


def iota(shape, dim):
    return lax.broadcasted_iota(jnp.int32, shape, dim)


def call(kernel, outs, *args, scratch=(), name=None):
    return pl.pallas_call(
        kernel,
        out_shape=outs,
        in_specs=[VMEM] * len(args),
        out_specs=jax.tree.map(lambda _: VMEM, outs),
        scratch_shapes=list(scratch),
        compiler_params=pltpu.CompilerParams(vmem_limit_bytes=40 * 1024 * 1024),
        name=name,
    )(*args)


def f32(*shape):
    return jax.ShapeDtypeStruct(shape, jnp.float32)


def picks():
    row, lane = iota((8, NJ), 0), iota((8, NJ), 1)
    want = jnp.where(row < 2, row, jnp.where(row < 4, NJ - 4 + row, -1))
    return jnp.where(lane == want, 1.0, 0.0).astype(jnp.float32)


def is_first():
    return lax.rem(lax.axis_index("gx"), lax.axis_size("gx") // 2) == 0


def is_last():
    half = lax.axis_size("gx") // 2
    return lax.rem(lax.axis_index("gx"), half) == half - 1


def pack_kernel(early, fields, diff, heights, to_a, to_b):
    @pl.when(is_first() == early)
    def _():
        even = lax.rem(lax.axis_index("gy"), 2) == 0
        rows = jnp.concatenate(
            [
                fields[...].reshape(NF * NZ * NI, NJ),
                diff[...].reshape(NZ * NI, NJ),
                heights[...].astype(jnp.float32),
                jnp.zeros((PACK - HEIGHT_AT - NI, NJ), jnp.float32),
            ],
            0,
        )
        cols = lax.dot_general(
            picks(), rows, (((1,), (1,)), ((), ())), precision=EXACT, preferred_element_type=jnp.float32
        )
        low, high = cols[0:2, :], cols[2:4, :]
        to_a[...] = jnp.where(even, high, low)
        to_b[...] = jnp.where(even, low, high)


def unpack_kernel(
    early_a, early_b, late_a, late_b, fields, diff, heights, halo, to_east, to_west, view
):
    even, early = lax.rem(lax.axis_index("gy"), 2) == 0, is_first()
    a = jnp.where(early, early_a[...], late_a[...])
    b = jnp.where(early, early_b[...], late_b[...])
    north, south = jnp.where(even, a, b), jnp.where(even, b, a)
    cols = jnp.concatenate([north, south, jnp.zeros((4, PACK), jnp.float32)], 0)
    spread = lax.dot_general(
        cols, picks(), (((0,), (0,)), ((), ())), precision=EXACT, preferred_element_type=jnp.float32
    )
    halo[...] = spread
    view[...] = spread[0:BLOCK, :].reshape(RIM, NI, NJ)
    spare = jnp.zeros((NJ - RIM, NJ), jnp.float32)
    for to, near, far in ((to_east, NI - 1, NI - 2), (to_west, 0, 1)):
        for i in range(NA):
            src = diff if i == NF else fields.at[i]
            to[i * NZ:(i + 1) * NZ, :] = src[:, near, :]
            to[RIM + i * NZ:RIM + (i + 1) * NZ, :] = src[:, far, :]
        row = heights[near:near + 1, :].astype(jnp.float32)
        to[2 * RIM:EDGE_ROWS, :] = jnp.broadcast_to(row, (8, NJ))
        corners = jnp.concatenate([view[:, near, :], spare], 0)
        to[EDGE_ROWS:MESSAGE, :] = lax.dot_general(
            picks(), corners, (((1,), (1,)), ((), ())), precision=EXACT, preferred_element_type=jnp.float32
        )


def levels(x, edge):
    k = iota(x.shape, 0)
    above = jnp.where(k == NZ - 1, x if edge else 0.0, pltpu.roll(x, NZ - 1, 0))
    below = jnp.where(k == 0, x if edge else 0.0, pltpu.roll(x, 1, 0))
    return above, below


def row_rates(near, far, height, sign):
    u, v, w = near[0], near[1], near[2]
    k_cell = near[NF]
    k_above, k_below = levels(k_cell, True)
    drag = jnp.where(iota(u.shape, 0).astype(jnp.float32) < height, DRAG_COEF, 0.0)
    resist = drag * jnp.sqrt(u * u + v * v + w * w + SPEED_EPS)
    rates = []
    for m in range(NF):
        f = near[m]
        above, below = levels(f, False)
        rate = 0.5 * (
            (k_cell + far[NF]) * (far[m] - f)
            + (k_cell + k_above) * (above - f)
            + (k_cell + k_below) * (below - f)
            + sign * u * far[m]
            - w * (above - below)
        )
        if m < 3:
            rate = rate - resist * f
        if m == 2:
            rate = rate + BUOYANCY * near[3]
        rates.append(rate)
    return rates


def split_rim(rim):
    near = [rim[a * NZ:(a + 1) * NZ, :] for a in range(NA)]
    far = [rim[RIM + a * NZ:RIM + (a + 1) * NZ, :] for a in range(NA)]
    return near, far, rim[2 * RIM:2 * RIM + 1, :]


def packet_kernel(fields_hbm, diff_hbm, heights_hbm, out, fields, diff, heights, sems):
    late = is_last()
    half = pl.ds(pl.multiple_of(jnp.where(late, NI - 8, 0), 8), 8)
    copies = [
        pltpu.make_async_copy(fields_hbm.at[:, :, half, :], fields, sems.at[0]),
        pltpu.make_async_copy(diff_hbm.at[:, half, :], diff, sems.at[1]),
        pltpu.make_async_copy(heights_hbm.at[half, :], heights, sems.at[2]),
    ]
    for copy in copies:
        copy.start()
    out[...] = jnp.zeros_like(out)
    for copy in copies:
        copy.wait()

    def row(r):
        both = [fields[m, :, r, :] for m in range(NF)], [fields[m, :, 7 - r, :] for m in range(NF)]
        parts = [jnp.where(late, b, a) for a, b in zip(*both)]
        return parts + [jnp.where(late, diff[:, 7 - r, :], diff[:, r, :])]

    near, far = row(0), row(1)
    height = jnp.where(late, heights[7:8, :], heights[0:1, :]).astype(jnp.float32)
    sign = jnp.where(late, 1.0, -1.0).astype(jnp.float32)
    rates = row_rates(near, far, height, sign)
    zero = jnp.zeros((NZ, NJ), jnp.float32)
    lower = [near[0], near[1], near[2], near[NF], rates[0], rates[1], rates[2], zero]
    upper = [near[3], near[4], near[1], near[NF], rates[3], rates[4], zero, zero]
    at = jnp.where(late, 0, 2 * NZ)
    for row in range(8):
        out[pl.ds(at, NZ), row, :] = lower[row]
        out[pl.ds(at + NZ, NZ), row, :] = upper[row]


def inverse_kernel(wrap, out):
    total = jnp.zeros((64, NJ), jnp.float32)
    lane = iota((32, NJ), 1).astype(jnp.float32)
    for s in range(32):
        p = wrap[s:s + 1, :]
        hit = jnp.where(iota((32, NJ), 0) == p // NJ, 1.0, 0.0)
        low = jnp.where(iota((NJ, NJ), 0) == lax.rem(p, NJ), 1.0, 0.0).astype(jnp.bfloat16)
        left = jnp.concatenate([hit * lane, hit * float(s)], 0).astype(jnp.bfloat16)
        total = total + lax.dot_general(
            left, low, (((1,), (1,)), ((), ())), preferred_element_type=jnp.float32
        )
    out[...] = (total[0:32, :] + NJ * total[32:64, :]).astype(jnp.int32)


def permute_kernel(rows, wrap, inverse, out, left_side, right_side):
    first, gx, half = is_first(), lax.axis_index("gx"), lax.axis_size("gx") // 2
    target = jnp.where(first, wrap[...], inverse[...])
    column = iota(target.shape, 0) * NJ + iota(target.shape, 1)
    target = jnp.where((gx == half) | (gx == half - 1), column, target)
    upper = lax.axis_index("gy") >= NZ
    x = jnp.where(first, rows[32:64], rows[0:32])
    lane, sub = iota(x.shape, 2), iota(x.shape, 1)

    def after(y):
        return jnp.concatenate([y[1:], y[:1]], 0)

    def before(y):
        return jnp.concatenate([y[-1:], y[:-1]], 0)

    left, right = pltpu.roll(x, NJ - 1, 2), pltpu.roll(x, 1, 2)
    north = jnp.where(lane == NJ - 1, after(left), left)
    south = jnp.where(lane == 0, before(right), right)
    v = jnp.where(upper, x[:, 2:3, :], x[:, 1:2, :])
    k_cell, k_north, k_south = x[:, 3:4, :], north[:, 3:4, :], south[:, 3:4, :]
    term = 0.5 * (
        (k_cell + k_north) * (north - x) + (k_cell + k_south) * (south - x) - v * (north - south)
    )
    x = x + jnp.where((sub >= 4) & (sub < 7), pltpu.roll(term, 4, 1), 0.0)

    part_a = x.astype(jnp.bfloat16).astype(jnp.float32)
    rest = x - part_a
    part_b = rest.astype(jnp.bfloat16).astype(jnp.float32)
    part_c = rest - part_b
    for s in range(32):
        t = target[s:s + 1, :]
        hi, lo = lax.shift_right_logical(t, 8), lax.bitwise_and(t, 255)
        stack = jnp.concatenate([part_a[s], part_b[s], part_c[s]], 0)
        masked = jnp.concatenate([jnp.where(hi == h, stack, 0.0) for h in range(16)], 0)
        at = slice(s * NJ, (s + 1) * NJ)
        left_side[:, at] = masked.astype(jnp.bfloat16)
        right_side[:, at] = jnp.where(iota((256, NJ), 0) == lo, 1.0, 0.0).astype(jnp.bfloat16)
    moved = lax.dot_general(
        left_side[...], right_side[...], (((1,), (1,)), ((), ())), preferred_element_type=jnp.float32
    )
    for h in range(16):
        at = h * 24
        tile = moved[at:at + 8, :] + moved[at + 8:at + 16, :] + moved[at + 16:at + 24, :]
        out[2 * h] = tile[:, 0:NJ]
        out[2 * h + 1] = tile[:, NJ:2 * NJ]
    y = out[...]
    prior, later = before(y), after(y)
    last = jnp.zeros_like(y)
    for r in range(4):
        corner = jnp.where(lane < 64, pltpu.roll(later, r, 2), pltpu.roll(prior, (NJ - r) % NJ, 2))
        corner = pltpu.roll(corner, 7 - r, 1)
        last = jnp.where((lane == r) | (lane == NJ - 1 - r), corner, last)
    out[...] = jnp.where(sub == 7, last, y)


def beside(m, h):
    lane = iota(m.shape, 1)
    m_left, h_left = pltpu.roll(m, NJ - 1, 1), pltpu.roll(h, NJ - 1, 1)
    m_right, h_right = pltpu.roll(m, 1, 1), pltpu.roll(h, 1, 1)
    at_end, at_start = lane == NJ - 1, lane == 0
    return (
        jnp.where(at_end, h_left, m_left),
        jnp.where(at_start, h_right, m_right),
        jnp.where(at_end, m_left, h_left),
        jnp.where(at_start, m_right, h_right),
    )


def rates_of(cells, k_cell, k_sides, drag, sign=None):
    u, v, w = cells[0][0], cells[1][0], cells[2][0]
    resist = drag * jnp.sqrt(u * u + v * v + w * w + SPEED_EPS)
    if sign is not None:
        u = sign * u
    sums = [k_cell + side for side in k_sides]
    total = sums[0] + sums[1] + sums[2] + sums[3] + sums[4] + sums[5]
    rates = []
    for m in range(NF):
        f, e, ws, n, s, up, dn = cells[m]
        rate = 0.5 * (
            (sums[0] - u) * e + (sums[1] + u) * ws
            + (sums[2] - v) * n + (sums[3] + v) * s
            + (sums[4] - w) * up + (sums[5] + w) * dn
            - total * f
        )
        if m < 3:
            rate = rate - resist * f
        if m == 2:
            rate = rate + BUOYANCY * cells[3][0]
        rates.append(rate)
    return rates


def sections_kernel(
    fields, diff, heights, west, east, halo, out, kept, one, one_halo, one_w, one_e, corner_w, corner_e
):
    first = is_first()
    sub = iota((NI, NJ), 0)

    for rim, sign, own_row, one_out, corners in (
        (west, 1.0, 0, one_w, corner_w), (east, -1.0, NI - 1, one_e, corner_e)
    ):
        corners[...] = lax.dot_general(
            rim[EDGE_ROWS:MESSAGE, :], picks(), (((0,), (0,)), ((), ())),
            precision=EXACT, preferred_element_type=jnp.float32,
        )
        near, far, height = split_rim(rim)
        rates = row_rates(near, far, height, sign)
        sides = [beside(near[i], corners[i * NZ:(i + 1) * NZ, :]) for i in range(NA)]
        k_cell, k_n, k_s = near[NF], sides[NF][0], sides[NF][1]
        k_own = diff[:, own_row, :]
        for m in range(NF):
            f, n, s = near[m], sides[m][0], sides[m][1]
            own = fields[m, :, own_row, :]
            rate = rates[m] + 0.5 * (
                (k_cell + k_n) * (n - f) + (k_cell + k_s) * (s - f) - near[1] * (n - s)
                + (k_cell + k_own) * (own - f) - sign * near[0] * own
            )
            one_out[m * NZ:(m + 1) * NZ, :] = f + TIME_STEP / 3.0 * rate

    def row_of(ref, i, k):
        return ref[pl.ds(i * NZ + k, 1), :]

    def along(x, low, high):
        return (
            jnp.where(sub == NI - 1, high, pltpu.roll(x, NI - 1, 0)),
            jnp.where(sub == 0, low, pltpu.roll(x, 1, 0)),
        )

    def halo_tile(i, k):
        at = pl.multiple_of((i * NZ + k) * NI, NI)
        return halo[pl.ds(at, NI), :]

    high_main = heights[...].astype(jnp.float32)
    high_halo = halo[HEIGHT_AT:HEIGHT_AT + NI, :]

    def section_one(k, _):
        up, dn = jnp.minimum(k + 1, NZ - 1), jnp.maximum(k - 1, 0)
        has_up = jnp.where(k < NZ - 1, 1.0, 0.0).astype(jnp.float32)
        has_dn = jnp.where(k > 0, 1.0, 0.0).astype(jnp.float32)
        level = k.astype(jnp.float32)
        k_main, k_halo = diff[k], halo_tile(NF, k)
        n, s, hn, hs = beside(k_main, k_halo)
        e, ws = along(k_main, row_of(west, NF, k), row_of(east, NF, k))
        he, hw = along(k_halo, row_of(corner_w, NF, k), row_of(corner_e, NF, k))
        k_sides = (e, ws, n, s, diff[up], diff[dn])
        kh_sides = (he, hw, hn, hs, halo_tile(NF, up), halo_tile(NF, dn))
        cells, halos = [], []
        for m in range(NF):
            f, h = fields[m, k], halo_tile(m, k)
            n, s, hn, hs = beside(f, h)
            e, ws = along(f, row_of(west, m, k), row_of(east, m, k))
            he, hw = along(h, row_of(corner_w, m, k), row_of(corner_e, m, k))
            cells.append((f, e, ws, n, s, has_up * fields[m, up], has_dn * fields[m, dn]))
            halos.append((h, he, hw, hn, hs, has_up * halo_tile(m, up), has_dn * halo_tile(m, dn)))
        drag = jnp.where(level < high_main, DRAG_COEF, 0.0)
        drag_h = jnp.where(level < high_halo, DRAG_COEF, 0.0)
        rates = rates_of(cells, k_main, k_sides, drag)
        rates_h = rates_of(halos, k_halo, kh_sides, drag_h)
        for m in range(NF):
            one[m, k] = cells[m][0] + TIME_STEP / 3.0 * rates[m]
            one_halo[m, k] = halos[m][0] + TIME_STEP / 3.0 * rates_h[m]
        return 0

    lax.fori_loop(0, NZ, section_one, 0)

    def section_two(k, _):
        up, dn = jnp.minimum(k + 1, NZ - 1), jnp.maximum(k - 1, 0)
        has_up = jnp.where(k < NZ - 1, 1.0, 0.0).astype(jnp.float32)
        has_dn = jnp.where(k > 0, 1.0, 0.0).astype(jnp.float32)
        k_main = diff[k]
        n, s, _, _ = beside(k_main, halo_tile(NF, k))
        e, ws = along(k_main, row_of(west, NF, k), row_of(east, NF, k))
        k_sides = (e, ws, n, s, diff[up], diff[dn])
        cells = []
        for m in range(NF):
            f = one[m, k]
            n, s, _, _ = beside(f, one_halo[m, k])
            e, ws = along(f, row_of(one_w, m, k), row_of(one_e, m, k))
            cells.append((f, e, ws, n, s, has_up * one[m, up], has_dn * one[m, dn]))
        drag = jnp.where(k.astype(jnp.float32) < high_main, DRAG_COEF, 0.0)
        rates = rates_of(cells, k_main, k_sides, drag)
        for m in range(NF):
            out[m, k] = fields[m, k] + TIME_STEP / 2.0 * rates[m]
        return 0

    lax.fori_loop(0, NZ, section_two, 0)
    for m in range(NF):
        for r in range(3):
            kept[m, r] = jnp.where(first, one[m, :, r, :], one[m, :, NI - 1 - r, :])
        for r in range(2):
            kept[m, 3 + r] = jnp.where(first, one_halo[m, :, r, :], one_halo[m, :, NI - 1 - r, :])


def wrap_kernel(fields, diff, heights, halo, kept, wrapped, done, out, view):
    first, final = is_first(), is_last()
    out[...] = done[...]

    @pl.when(first | final)
    def _():
        view[...] = halo[0:BLOCK, :].reshape(RIM, NI, NJ)
        sign = jnp.where(first, 1.0, -1.0).astype(jnp.float32)
        lane = iota((NZ, NJ), 1)

        def block_row(i, r):
            src = diff if i == NF else fields.at[i]
            return jnp.where(first, src[:, r, :], src[:, NI - 1 - r, :])

        def halo_row(i, r):
            at = slice(i * NZ, (i + 1) * NZ)
            return jnp.where(first, view[at, r, :], view[at, NI - 1 - r, :])

        place = {0: (0, 0), 1: (0, 1), 2: (0, 2), NF: (0, 3), 3: (NZ, 0), 4: (NZ, 1)}
        outer, corner = [], []
        for i in range(NA):
            half, row = place[i]
            outer.append(wrapped[half:half + NZ, row, :])
            spare = wrapped[half:half + NZ, 7, :]
            corner.append(
                jnp.where(lane < 64, pltpu.roll(spare, (NJ - row) % NJ, 1), pltpu.roll(spare, row, 1))
            )
        own = [block_row(i, 0) for i in range(NA)]
        side = [halo_row(i, 0) for i in range(NA)]
        one_out, one_own, one_side = [], [], []
        for m in range(NF):
            half, row = (0, 4 + m) if m < 3 else (NZ, 1 + m)
            rate = wrapped[half:half + NZ, row, :] + 0.5 * (
                (outer[NF] + own[NF]) * (own[m] - outer[m]) - sign * outer[0] * own[m]
            )
            one_out.append(outer[m] + TIME_STEP / 3.0 * rate)
            rate = (own[NF] + outer[NF] + sign * own[0]) * outer[m] - outer[NF] * own[m]
            one_own.append(kept[m, 0] + TIME_STEP / 6.0 * rate)
            rate = (side[NF] + corner[NF] + sign * side[0]) * corner[m] - corner[NF] * side[m]
            one_side.append(kept[m, 3] + TIME_STEP / 6.0 * rate)
        k_rows = [outer[NF], own[NF], block_row(NF, 1), block_row(NF, 2)]
        k_halos = [side[NF], halo_row(NF, 1)]
        ones = [[one_out[m], one_own[m], kept[m, 1], kept[m, 2]] for m in range(NF)]
        one_halos = [[one_side[m], kept[m, 4]] for m in range(NF)]
        for r in range(2):
            k_cell = k_rows[r + 1]
            k_n, k_s, _, _ = beside(k_cell, k_halos[r])
            k_up, k_dn = levels(k_cell, True)
            k_sides = (k_rows[r + 2], k_rows[r], k_n, k_s, k_up, k_dn)
            cells = []
            for m in range(NF):
                f = ones[m][r + 1]
                n, s, _, _ = beside(f, one_halos[m][r])
                up, dn = levels(f, False)
                cells.append((f, ones[m][r + 2], ones[m][r], n, s, up, dn))
            height = jnp.where(first, heights[r:r + 1, :], heights[NI - 1 - r:NI - r, :])
            drag = jnp.where(iota((NZ, NJ), 0) < height, DRAG_COEF, 0.0)
            rates = rates_of(cells, k_cell, k_sides, drag, sign)
            for m in range(NF):
                value = block_row(m, r) + TIME_STEP / 2.0 * rates[m]

                @pl.when(first)
                def _(value=value, m=m):
                    out[m, :, r, :] = value

                @pl.when(final)
                def _(value=value, m=m):
                    out[m, :, NI - 1 - r, :] = value


def shards(fields, diffusivity, heights, wrap_map):
    count_x, count_y = lax.axis_size("gx"), lax.axis_size("gy")
    last = count_x - 1
    pack = f32(2, PACK)
    block = (fields, diffusivity, heights)
    half = pltpu.VMEM((NF, NZ, 8, NJ), jnp.float32), pltpu.VMEM((NZ, 8, NJ), jnp.float32)
    packets = pl.pallas_call(
        packet_kernel,
        out_shape=f32(2 * count_y, 8, NJ),
        in_specs=[pl.BlockSpec(memory_space=pl.ANY)] * 3,
        out_specs=VMEM,
        scratch_shapes=[*half, pltpu.VMEM((8, NJ), jnp.int32), pltpu.SemaphoreType.DMA((3,))],
        compiler_params=pltpu.CompilerParams(vmem_limit_bytes=56 * 1024 * 1024),
        name="packets",
    )(*block)

    half_x = count_x // 2
    early_rows = [0, half_x]
    rest = [r for r in range(count_x) if r not in early_rows]
    low = [(i, i + 1) for i in range(0, count_y, 2)]
    high = [(i, (i + 1) % count_y) for i in range(1, count_y, 2)]

    def spanwise(early, rows, *after):
        tied = lax.optimization_barrier((*block, *after))[:3]
        to_a, to_b = call(functools.partial(pack_kernel, early), (pack, pack), *tied, name="pack")

        def swap(x, pairs):
            pairs = [(r * count_y + i, r * count_y + j) for r in rows for i, j in pairs]
            return lax.ppermute(x, ("gx", "gy"), pairs + [(j, i) for i, j in pairs])

        from_b = swap(to_b, high)
        return swap(to_a, low), from_b

    early_a, early_b = spanwise(True, early_rows, packets)
    packets, early_a, early_b = lax.optimization_barrier((packets, early_a, early_b))

    row_pairs = [(0, last), (half_x, half_x - 1)] + [(i, i + half_x) for i in range(1, half_x - 1)]
    groups = [[r * count_y + i for r in rows for i in range(count_y)] for rows in row_pairs]
    rows = lax.all_to_all(packets, ("gx", "gy"), 0, 0, axis_index_groups=groups)

    late_a, late_b = spanwise(False, rest, packets)
    message = f32(MESSAGE, NJ)
    halo, to_east, to_west = call(
        unpack_kernel, (f32(PACK, NJ), message, message),
        early_a, early_b, late_a, late_b, *block, name="unpack",
        scratch=[pltpu.VMEM((RIM, NI, NJ), jnp.float32)],
    )
    east_pairs = [(i, i + 1) for i in range(last) if i + 1 != half_x]
    west = lax.ppermute(to_east, "gx", east_pairs)
    east = lax.ppermute(to_west, "gx", [(j, i) for i, j in east_pairs])

    wrap = wrap_map.reshape(count_y, NJ)
    inverse = call(
        inverse_kernel, jax.ShapeDtypeStruct((count_y, NJ), jnp.int32), wrap, name="inverse"
    )
    rows, inverse, *_ = lax.optimization_barrier((rows, inverse, to_east, to_west))
    moved = call(
        permute_kernel, f32(count_y, 8, NJ), rows, wrap, inverse, name="permute",
        scratch=[pltpu.VMEM((384, 32 * NJ), jnp.bfloat16), pltpu.VMEM((256, 32 * NJ), jnp.bfloat16)],
    )
    moved, west, east = lax.optimization_barrier((moved, west, east))
    wrapped = lax.all_to_all(moved, "gy", 0, 0)

    state = pltpu.VMEM((NF, NZ, NI, NJ), jnp.float32)
    line = pltpu.VMEM((RIM, NJ), jnp.float32)
    corner = pltpu.VMEM((NJ, NJ), jnp.float32)
    done, kept = call(
        sections_kernel, (f32(NF, NZ, NI, NJ), f32(NF, 5, NZ, NJ)),
        *block, west, east, halo, name="sections", scratch=[state, state, line, line, corner, corner],
    )
    return call(
        wrap_kernel, f32(NF, NZ, NI, NJ), *block, halo, kept, wrapped, done, name="wrapped_rows",
        scratch=[pltpu.VMEM((RIM, NI, NJ), jnp.float32)],
    )


def solution(mesh):
    in_specs = (P(None, None, "gx", "gy"), P(None, "gx", "gy"), P("gx", "gy"), P())
    out_specs = P(None, None, "gx", "gy")
    return jax.shard_map(shards, mesh=mesh, in_specs=in_specs, out_specs=out_specs, check_vma=False)
```

```python
import jax
import jax.numpy as jnp
from jax import lax
from jax.experimental import pallas as pl
from jax.experimental.pallas import tpu as pltpu
from jax.sharding import PartitionSpec as P

DRAG_COEF = 1.0
TIME_STEP = 0.3
BUOYANCY = 0.5
SPEED_EPS = 0.01

NF = 5
NA = 6
NZ = 16
NI = 16
NJ = 128
RIM = NA * NZ
EDGE_ROWS = 2 * RIM + 8
MESSAGE = EDGE_ROWS + 8
BLOCK = NA * NZ * NI
PACK = BLOCK + 128
HEIGHT_AT = BLOCK
HALO = RIM + 1

VMEM = pl.BlockSpec(memory_space=pltpu.VMEM)
EXACT = lax.Precision.HIGHEST


def iota(shape, dim):
    return lax.broadcasted_iota(jnp.int32, shape, dim)


def call(kernel, outs, *args, scratch=(), name=None):
    return pl.pallas_call(
        kernel,
        out_shape=outs,
        in_specs=[VMEM] * len(args),
        out_specs=jax.tree.map(lambda _: VMEM, outs),
        scratch_shapes=list(scratch),
        compiler_params=pltpu.CompilerParams(vmem_limit_bytes=40 * 1024 * 1024),
        name=name,
    )(*args)


def f32(*shape):
    return jax.ShapeDtypeStruct(shape, jnp.float32)


def picks():
    row, lane = iota((8, NJ), 0), iota((8, NJ), 1)
    want = jnp.where(row < 2, row, jnp.where(row < 4, NJ - 4 + row, -1))
    return jnp.where(lane == want, 1.0, 0.0).astype(jnp.float32)


def is_first():
    return lax.rem(lax.axis_index("gx"), lax.axis_size("gx") // 2) == 0


def is_last():
    half = lax.axis_size("gx") // 2
    return lax.rem(lax.axis_index("gx"), half) == half - 1


def pack_kernel(fields, diff, heights, to_a, to_b):
    even = lax.rem(lax.axis_index("gy"), 2) == 0
    rows = jnp.concatenate(
        [
            fields[...].reshape(NF * NZ * NI, NJ),
            diff[...].reshape(NZ * NI, NJ),
            heights[...].astype(jnp.float32),
            jnp.zeros((PACK - HEIGHT_AT - NI, NJ), jnp.float32),
        ],
        0,
    )
    cols = lax.dot_general(
        picks(), rows, (((1,), (1,)), ((), ())), precision=EXACT, preferred_element_type=jnp.float32
    )
    low, high = cols[0:2, :], cols[2:4, :]
    to_a[...] = jnp.where(even, high, low)
    to_b[...] = jnp.where(even, low, high)


def unpack_kernel(from_a, from_b, fields, diff, heights, halo, to_east, to_west):
    even = lax.rem(lax.axis_index("gy"), 2) == 0
    a, b = from_a[...], from_b[...]
    north, south = jnp.where(even, a, b), jnp.where(even, b, a)
    cols = jnp.concatenate([north, south, jnp.zeros((4, PACK), jnp.float32)], 0)
    spread = lax.dot_general(
        cols, picks(), (((0,), (0,)), ((), ())), precision=EXACT, preferred_element_type=jnp.float32
    )
    halo[...] = spread[0:HALO * NI, :].reshape(HALO, NI, NJ)
    spare = jnp.zeros((NJ - RIM, NJ), jnp.float32)
    for to, near, far in ((to_east, NI - 1, NI - 2), (to_west, 0, 1)):
        for i in range(NA):
            src = diff if i == NF else fields.at[i]
            to[i * NZ:(i + 1) * NZ, :] = src[:, near, :]
            to[RIM + i * NZ:RIM + (i + 1) * NZ, :] = src[:, far, :]
        row = heights[near:near + 1, :].astype(jnp.float32)
        to[2 * RIM:EDGE_ROWS, :] = jnp.broadcast_to(row, (8, NJ))
        corners = jnp.concatenate([halo[0:RIM, near, :], spare], 0)
        to[EDGE_ROWS:MESSAGE, :] = lax.dot_general(
            picks(), corners, (((1,), (1,)), ((), ())), precision=EXACT, preferred_element_type=jnp.float32
        )


def levels(x, edge):
    k = iota(x.shape, 0)
    above = jnp.where(k == NZ - 1, x if edge else 0.0, pltpu.roll(x, NZ - 1, 0))
    below = jnp.where(k == 0, x if edge else 0.0, pltpu.roll(x, 1, 0))
    return above, below


def row_rates(near, far, height, sign):
    u, v, w = near[0], near[1], near[2]
    k_cell = near[NF]
    k_above, k_below = levels(k_cell, True)
    drag = jnp.where(iota(u.shape, 0).astype(jnp.float32) < height, DRAG_COEF, 0.0)
    resist = drag * jnp.sqrt(u * u + v * v + w * w + SPEED_EPS)
    rates = []
    for m in range(NF):
        f = near[m]
        above, below = levels(f, False)
        rate = 0.5 * (
            (k_cell + far[NF]) * (far[m] - f)
            + (k_cell + k_above) * (above - f)
            + (k_cell + k_below) * (below - f)
            + sign * u * far[m]
            - w * (above - below)
        )
        if m < 3:
            rate = rate - resist * f
        if m == 2:
            rate = rate + BUOYANCY * near[3]
        rates.append(rate)
    return rates


def split_rim(rim):
    near = [rim[a * NZ:(a + 1) * NZ, :] for a in range(NA)]
    far = [rim[RIM + a * NZ:RIM + (a + 1) * NZ, :] for a in range(NA)]
    return near, far, rim[2 * RIM:2 * RIM + 1, :]


def packet_kernel(fields_hbm, diff_hbm, heights_hbm, out, fields, diff, heights, sems):
    late = is_last()
    half = pl.ds(pl.multiple_of(jnp.where(late, NI - 8, 0), 8), 8)
    copies = [
        pltpu.make_async_copy(fields_hbm.at[:, :, half, :], fields, sems.at[0]),
        pltpu.make_async_copy(diff_hbm.at[:, half, :], diff, sems.at[1]),
        pltpu.make_async_copy(heights_hbm.at[half, :], heights, sems.at[2]),
    ]
    for copy in copies:
        copy.start()
    out[...] = jnp.zeros_like(out)
    for copy in copies:
        copy.wait()

    def row(r):
        both = [fields[m, :, r, :] for m in range(NF)], [fields[m, :, 7 - r, :] for m in range(NF)]
        parts = [jnp.where(late, b, a) for a, b in zip(*both)]
        return parts + [jnp.where(late, diff[:, 7 - r, :], diff[:, r, :])]

    near, far = row(0), row(1)
    height = jnp.where(late, heights[7:8, :], heights[0:1, :]).astype(jnp.float32)
    sign = jnp.where(late, 1.0, -1.0).astype(jnp.float32)
    rates = row_rates(near, far, height, sign)
    zero = jnp.zeros((NZ, NJ), jnp.float32)
    lower = [near[0], near[1], near[2], near[NF], rates[0], rates[1], rates[2], zero]
    upper = [near[3], near[4], near[1], near[NF], rates[3], rates[4], zero, zero]
    at = jnp.where(late, 0, 2 * NZ)
    for row in range(8):
        out[pl.ds(at, NZ), row, :] = lower[row]
        out[pl.ds(at + NZ, NZ), row, :] = upper[row]


def inverse_kernel(wrap, out):
    total = jnp.zeros((64, NJ), jnp.float32)
    lane = iota((32, NJ), 1).astype(jnp.float32)
    for s in range(32):
        p = wrap[s:s + 1, :]
        hit = jnp.where(iota((32, NJ), 0) == p // NJ, 1.0, 0.0)
        low = jnp.where(iota((NJ, NJ), 0) == lax.rem(p, NJ), 1.0, 0.0).astype(jnp.bfloat16)
        left = jnp.concatenate([hit * lane, hit * float(s)], 0).astype(jnp.bfloat16)
        total = total + lax.dot_general(
            left, low, (((1,), (1,)), ((), ())), preferred_element_type=jnp.float32
        )
    out[...] = (total[0:32, :] + NJ * total[32:64, :]).astype(jnp.int32)


def permute_kernel(rows, wrap, inverse, out, left_side, right_side):
    first, gx, half = is_first(), lax.axis_index("gx"), lax.axis_size("gx") // 2
    target = jnp.where(first, wrap[...], inverse[...])
    column = iota(target.shape, 0) * NJ + iota(target.shape, 1)
    target = jnp.where((gx == half) | (gx == half - 1), column, target)
    upper = lax.axis_index("gy") >= NZ
    x = jnp.where(first, rows[32:64], rows[0:32])
    lane, sub = iota(x.shape, 2), iota(x.shape, 1)

    def after(y):
        return jnp.concatenate([y[1:], y[:1]], 0)

    def before(y):
        return jnp.concatenate([y[-1:], y[:-1]], 0)

    left, right = pltpu.roll(x, NJ - 1, 2), pltpu.roll(x, 1, 2)
    north = jnp.where(lane == NJ - 1, after(left), left)
    south = jnp.where(lane == 0, before(right), right)
    v = jnp.where(upper, x[:, 2:3, :], x[:, 1:2, :])
    k_cell, k_north, k_south = x[:, 3:4, :], north[:, 3:4, :], south[:, 3:4, :]
    term = 0.5 * (
        (k_cell + k_north) * (north - x) + (k_cell + k_south) * (south - x) - v * (north - south)
    )
    x = x + jnp.where((sub >= 4) & (sub < 7), pltpu.roll(term, 4, 1), 0.0)

    part_a = x.astype(jnp.bfloat16).astype(jnp.float32)
    rest = x - part_a
    part_b = rest.astype(jnp.bfloat16).astype(jnp.float32)
    part_c = rest - part_b
    for s in range(32):
        t = target[s:s + 1, :]
        hi, lo = lax.shift_right_logical(t, 8), lax.bitwise_and(t, 255)
        stack = jnp.concatenate([part_a[s], part_b[s], part_c[s]], 0)
        masked = jnp.concatenate([jnp.where(hi == h, stack, 0.0) for h in range(16)], 0)
        at = slice(s * NJ, (s + 1) * NJ)
        left_side[:, at] = masked.astype(jnp.bfloat16)
        right_side[:, at] = jnp.where(iota((256, NJ), 0) == lo, 1.0, 0.0).astype(jnp.bfloat16)
    moved = lax.dot_general(
        left_side[...], right_side[...], (((1,), (1,)), ((), ())), preferred_element_type=jnp.float32
    )
    for h in range(16):
        at = h * 24
        tile = moved[at:at + 8, :] + moved[at + 8:at + 16, :] + moved[at + 16:at + 24, :]
        out[2 * h] = tile[:, 0:NJ]
        out[2 * h + 1] = tile[:, NJ:2 * NJ]
    y = out[...]
    prior, later = before(y), after(y)
    last = jnp.zeros_like(y)
    for r in range(4):
        corner = jnp.where(lane < 64, pltpu.roll(later, r, 2), pltpu.roll(prior, (NJ - r) % NJ, 2))
        corner = pltpu.roll(corner, 7 - r, 1)
        last = jnp.where((lane == r) | (lane == NJ - 1 - r), corner, last)
    out[...] = jnp.where(sub == 7, last, y)


def beside(m, h):
    lane = iota(m.shape, 1)
    m_left, h_left = pltpu.roll(m, NJ - 1, 1), pltpu.roll(h, NJ - 1, 1)
    m_right, h_right = pltpu.roll(m, 1, 1), pltpu.roll(h, 1, 1)
    at_end, at_start = lane == NJ - 1, lane == 0
    return (
        jnp.where(at_end, h_left, m_left),
        jnp.where(at_start, h_right, m_right),
        jnp.where(at_end, m_left, h_left),
        jnp.where(at_start, m_right, h_right),
    )


def rates_of(cells, k_cell, k_sides, drag, sign=None):
    u, v, w = cells[0][0], cells[1][0], cells[2][0]
    resist = drag * jnp.sqrt(u * u + v * v + w * w + SPEED_EPS)
    if sign is not None:
        u = sign * u
    sums = [k_cell + side for side in k_sides]
    total = sums[0] + sums[1] + sums[2] + sums[3] + sums[4] + sums[5]
    rates = []
    for m in range(NF):
        f, e, ws, n, s, up, dn = cells[m]
        rate = 0.5 * (
            (sums[0] - u) * e + (sums[1] + u) * ws
            + (sums[2] - v) * n + (sums[3] + v) * s
            + (sums[4] - w) * up + (sums[5] + w) * dn
            - total * f
        )
        if m < 3:
            rate = rate - resist * f
        if m == 2:
            rate = rate + BUOYANCY * cells[3][0]
        rates.append(rate)
    return rates


def sections_kernel(fields, diff, heights, halo, out, kept, one, one_halo):
    sub = iota((NI, NJ), 0)

    def along(x):
        return (
            jnp.where(sub == NI - 1, 0.0, pltpu.roll(x, NI - 1, 0)),
            jnp.where(sub == 0, 0.0, pltpu.roll(x, 1, 0)),
        )

    high_main = heights[...].astype(jnp.float32)
    high_halo = halo[HALO - 1]

    def section_one(k, _):
        up, dn = jnp.minimum(k + 1, NZ - 1), jnp.maximum(k - 1, 0)
        has_up = jnp.where(k < NZ - 1, 1.0, 0.0).astype(jnp.float32)
        has_dn = jnp.where(k > 0, 1.0, 0.0).astype(jnp.float32)
        level = k.astype(jnp.float32)
        k_main, k_halo = diff[k], halo[NF * NZ + k]
        n, s, hn, hs = beside(k_main, k_halo)
        k_sides = (*along(k_main), n, s, diff[up], diff[dn])
        kh_sides = (*along(k_halo), hn, hs, halo[NF * NZ + up], halo[NF * NZ + dn])
        cells, halos = [], []
        for m in range(NF):
            f, h = fields[m, k], halo[m * NZ + k]
            n, s, hn, hs = beside(f, h)
            cells.append((f, *along(f), n, s, has_up * fields[m, up], has_dn * fields[m, dn]))
            halos.append((h, *along(h), hn, hs, has_up * halo[m * NZ + up], has_dn * halo[m * NZ + dn]))
        drag = jnp.where(level < high_main, DRAG_COEF, 0.0)
        drag_h = jnp.where(level < high_halo, DRAG_COEF, 0.0)
        rates = rates_of(cells, k_main, k_sides, drag)
        rates_h = rates_of(halos, k_halo, kh_sides, drag_h)
        for m in range(NF):
            one[m, k] = cells[m][0] + TIME_STEP / 3.0 * rates[m]
            one_halo[m, k] = halos[m][0] + TIME_STEP / 3.0 * rates_h[m]
        return 0

    lax.fori_loop(0, NZ, section_one, 0)

    def section_two(k, _):
        up, dn = jnp.minimum(k + 1, NZ - 1), jnp.maximum(k - 1, 0)
        has_up = jnp.where(k < NZ - 1, 1.0, 0.0).astype(jnp.float32)
        has_dn = jnp.where(k > 0, 1.0, 0.0).astype(jnp.float32)
        k_main = diff[k]
        n, s, _, _ = beside(k_main, halo[NF * NZ + k])
        k_sides = (*along(k_main), n, s, diff[up], diff[dn])
        cells = []
        for m in range(NF):
            f = one[m, k]
            n, s, _, _ = beside(f, one_halo[m, k])
            cells.append((f, *along(f), n, s, has_up * one[m, up], has_dn * one[m, dn]))
        drag = jnp.where(k.astype(jnp.float32) < high_main, DRAG_COEF, 0.0)
        rates = rates_of(cells, k_main, k_sides, drag)
        for m in range(NF):
            out[m, k] = fields[m, k] + TIME_STEP / 2.0 * rates[m]
        return 0

    lax.fori_loop(0, NZ, section_two, 0)
    for m in range(NF):
        for r in range(3):
            kept[0, m, r] = one[m, :, r, :]
            kept[1, m, r] = one[m, :, NI - 1 - r, :]
        for r in range(2):
            kept[0, m, 3 + r] = one_halo[m, :, r, :]
            kept[1, m, 3 + r] = one_halo[m, :, NI - 1 - r, :]


def edges_kernel(fields, diff, heights, halo, kept, west, east, wrapped, done, out):
    out[...] = done[...]
    lane = iota((NZ, NJ), 1)
    place = {0: (0, 0), 1: (0, 1), 2: (0, 2), NF: (0, 3), 3: (NZ, 0), 4: (NZ, 1)}

    for side, rim, mine, sign in ((0, west, is_first(), 1.0), (1, east, is_last(), -1.0)):
        rows = [r if side == 0 else NI - 1 - r for r in range(3)]

        def block_row(i, r):
            return (diff if i == NF else fields.at[i])[:, rows[r], :]

        def halo_row(i, r):
            return halo[i * NZ:(i + 1) * NZ, rows[r], :]

        outer, far, height = split_rim(rim)
        rates = row_rates(outer, far, height, sign)
        corner = lax.dot_general(
            rim[EDGE_ROWS:MESSAGE, :], picks(), (((0,), (0,)), ((), ())),
            precision=EXACT, preferred_element_type=jnp.float32,
        )
        corner = [corner[i * NZ:(i + 1) * NZ, :] for i in range(NA)]
        sides = [beside(outer[i], corner[i]) for i in range(NA)]
        k_cell, k_n, k_s = outer[NF], sides[NF][0], sides[NF][1]
        for m in range(NF):
            f, n, s = outer[m], sides[m][0], sides[m][1]
            rate = rates[m] + 0.5 * ((k_cell + k_n) * (n - f) + (k_cell + k_s) * (s - f) - outer[1] * (n - s))
            half, row = (0, 4 + m) if m < 3 else (NZ, 1 + m)
            rates[m] = jnp.where(mine, wrapped[half:half + NZ, row, :], rate)
        for i in range(NA):
            half, row = place[i]
            outer[i] = jnp.where(mine, wrapped[half:half + NZ, row, :], outer[i])
            spare = wrapped[half:half + NZ, 7, :]
            spare = jnp.where(lane < 64, pltpu.roll(spare, (NJ - row) % NJ, 1), pltpu.roll(spare, row, 1))
            corner[i] = jnp.where(mine, spare, corner[i])
        own = [block_row(i, 0) for i in range(NA)]
        beyond = [halo_row(i, 0) for i in range(NA)]
        ones, one_halos = [], []
        for m in range(NF):
            rate = rates[m] + 0.5 * (
                (outer[NF] + own[NF]) * (own[m] - outer[m]) - sign * outer[0] * own[m]
            )
            one_out = outer[m] + TIME_STEP / 3.0 * rate
            rate = (own[NF] + outer[NF] + sign * own[0]) * outer[m] - outer[NF] * own[m]
            one_own = kept[side, m, 0] + TIME_STEP / 6.0 * rate
            rate = (beyond[NF] + corner[NF] + sign * beyond[0]) * corner[m] - corner[NF] * beyond[m]
            ones.append([one_out, one_own, kept[side, m, 1], kept[side, m, 2]])
            one_halos.append([kept[side, m, 3] + TIME_STEP / 6.0 * rate, kept[side, m, 4]])
        k_rows = [outer[NF], own[NF], block_row(NF, 1), block_row(NF, 2)]
        k_halos = [beyond[NF], halo_row(NF, 1)]
        for r in range(2):
            k_cell = k_rows[r + 1]
            k_n, k_s, _, _ = beside(k_cell, k_halos[r])
            k_sides = (k_rows[r + 2], k_rows[r], k_n, k_s, *levels(k_cell, True))
            cells = []
            for m in range(NF):
                f = ones[m][r + 1]
                n, s, _, _ = beside(f, one_halos[m][r])
                cells.append((f, ones[m][r + 2], ones[m][r], n, s, *levels(f, False)))
            drag = jnp.where(iota((NZ, NJ), 0) < heights[rows[r]:rows[r] + 1, :], DRAG_COEF, 0.0)
            rates = rates_of(cells, k_cell, k_sides, drag, sign)
            for m in range(NF):
                out[m, :, rows[r], :] = block_row(m, r) + TIME_STEP / 2.0 * rates[m]


def shards(fields, diffusivity, heights, wrap_map):
    count_x, count_y = lax.axis_size("gx"), lax.axis_size("gy")
    last = count_x - 1
    pack = f32(2, PACK)
    block = (fields, diffusivity, heights)
    half = pltpu.VMEM((NF, NZ, 8, NJ), jnp.float32), pltpu.VMEM((NZ, 8, NJ), jnp.float32)
    packets = pl.pallas_call(
        packet_kernel,
        out_shape=f32(2 * count_y, 8, NJ),
        in_specs=[pl.BlockSpec(memory_space=pl.ANY)] * 3,
        out_specs=VMEM,
        scratch_shapes=[*half, pltpu.VMEM((8, NJ), jnp.int32), pltpu.SemaphoreType.DMA((3,))],
        compiler_params=pltpu.CompilerParams(vmem_limit_bytes=56 * 1024 * 1024),
        name="packets",
    )(*block)

    half_x = count_x // 2
    row_pairs = [(0, last), (half_x, half_x - 1)] + [(i, i + half_x) for i in range(1, half_x - 1)]
    groups = [[r * count_y + i for r in rows for i in range(count_y)] for rows in row_pairs]
    rows = lax.all_to_all(packets, ("gx", "gy"), 0, 0, axis_index_groups=groups)

    low = [(i, i + 1) for i in range(0, count_y, 2)]
    high = [(i, (i + 1) % count_y) for i in range(1, count_y, 2)]
    tied = lax.optimization_barrier((*block, packets))[:3]
    to_a, to_b = call(pack_kernel, (pack, pack), *tied, name="pack")
    from_b = lax.ppermute(to_b, "gy", high + [(j, i) for i, j in high])
    from_a = lax.ppermute(to_a, "gy", low + [(j, i) for i, j in low])

    wrap = wrap_map.reshape(count_y, NJ)
    inverse = call(
        inverse_kernel, jax.ShapeDtypeStruct((count_y, NJ), jnp.int32), wrap, name="inverse"
    )
    rows, inverse, from_a, from_b = lax.optimization_barrier((rows, inverse, from_a, from_b))
    moved = call(
        permute_kernel, f32(count_y, 8, NJ), rows, wrap, inverse, name="permute",
        scratch=[pltpu.VMEM((384, 32 * NJ), jnp.bfloat16), pltpu.VMEM((256, 32 * NJ), jnp.bfloat16)],
    )
    wrapped = lax.all_to_all(moved, "gy", 0, 0)

    message = f32(MESSAGE, NJ)
    halo, to_east, to_west = call(
        unpack_kernel, (f32(HALO, NI, NJ), message, message),
        from_a, from_b, *block, name="unpack",
            )
    east_pairs = [(i, i + 1) for i in range(last) if i + 1 != half_x]
    west = lax.ppermute(to_east, "gx", east_pairs)
    east = lax.ppermute(to_west, "gx", [(j, i) for i, j in east_pairs])

    state = pltpu.VMEM((NF, NZ, NI, NJ), jnp.float32)
    done, kept = call(
        sections_kernel, (f32(NF, NZ, NI, NJ), f32(2, NF, 5, NZ, NJ)),
        *block, halo, name="sections", scratch=[state, state],
    )
    return call(
        edges_kernel, f32(NF, NZ, NI, NJ), *block, halo, kept, west, east, wrapped, done, name="edges"
    )


def solution(mesh):
    in_specs = (P(None, None, "gx", "gy"), P(None, "gx", "gy"), P("gx", "gy"), P())
    out_specs = P(None, None, "gx", "gy")
    return jax.shard_map(shards, mesh=mesh, in_specs=in_specs, out_specs=out_specs, check_vma=False)
```

```python
import jax
import jax.numpy as jnp
from jax import lax
from jax.experimental import pallas as pl
from jax.experimental.pallas import tpu as pltpu
from jax.sharding import PartitionSpec as P

DRAG_COEF = 1.0
TIME_STEP = 0.3
BUOYANCY = 0.5
SPEED_EPS = 0.01

NF = 5
NA = 6
NZ = 16
NI = 16
NJ = 128
RIM = NA * NZ
EDGE_ROWS = 2 * RIM + 8
MESSAGE = EDGE_ROWS + 8
BLOCK = NA * NZ * NI
PACK = BLOCK + 128
HEIGHT_AT = BLOCK
HALO = RIM + 1

LEAD = 16

VMEM = pl.BlockSpec(memory_space=pltpu.VMEM)
EXACT = lax.Precision.HIGHEST


def iota(shape, dim):
    return lax.broadcasted_iota(jnp.int32, shape, dim)


def call(kernel, outs, *args, scratch=(), name=None):
    return pl.pallas_call(
        kernel,
        out_shape=outs,
        in_specs=[VMEM] * len(args),
        out_specs=jax.tree.map(lambda _: VMEM, outs),
        scratch_shapes=list(scratch),
        compiler_params=pltpu.CompilerParams(vmem_limit_bytes=40 * 1024 * 1024),
        name=name,
    )(*args)


def f32(*shape):
    return jax.ShapeDtypeStruct(shape, jnp.float32)


def picks():
    row, lane = iota((8, NJ), 0), iota((8, NJ), 1)
    want = jnp.where(row < 2, row, jnp.where(row < 4, NJ - 4 + row, -1))
    return jnp.where(lane == want, 1.0, 0.0).astype(jnp.float32)


def is_first():
    return lax.rem(lax.axis_index("gx"), lax.axis_size("gx") // 2) == 0


def is_last():
    half = lax.axis_size("gx") // 2
    return lax.rem(lax.axis_index("gx"), half) == half - 1


def pack_kernel(fields, diff, heights, to_a, to_b):
    even = lax.rem(lax.axis_index("gy"), 2) == 0
    rows = jnp.concatenate(
        [
            fields[...].reshape(NF * NZ * NI, NJ),
            diff[...].reshape(NZ * NI, NJ),
            heights[...].astype(jnp.float32),
            jnp.zeros((PACK - HEIGHT_AT - NI, NJ), jnp.float32),
        ],
        0,
    )
    cols = lax.dot_general(
        picks(), rows, (((1,), (1,)), ((), ())), precision=EXACT, preferred_element_type=jnp.float32
    )
    low, high = cols[0:2, :], cols[2:4, :]
    to_a[...] = jnp.where(even, high, low)
    to_b[...] = jnp.where(even, low, high)


def unpack_kernel(from_a, from_b, fields, diff, heights, halo, to_east, to_west):
    even = lax.rem(lax.axis_index("gy"), 2) == 0
    a, b = from_a[...], from_b[...]
    north, south = jnp.where(even, a, b), jnp.where(even, b, a)
    cols = jnp.concatenate([north, south, jnp.zeros((4, PACK), jnp.float32)], 0)
    spread = lax.dot_general(
        cols, picks(), (((0,), (0,)), ((), ())), precision=EXACT, preferred_element_type=jnp.float32
    )
    halo[...] = spread[0:HALO * NI, :].reshape(HALO, NI, NJ)
    spare = jnp.zeros((NJ - RIM, NJ), jnp.float32)
    for to, near, far in ((to_east, NI - 1, NI - 2), (to_west, 0, 1)):
        for i in range(NA):
            src = diff if i == NF else fields.at[i]
            to[i * NZ:(i + 1) * NZ, :] = src[:, near, :]
            to[RIM + i * NZ:RIM + (i + 1) * NZ, :] = src[:, far, :]
        row = heights[near:near + 1, :].astype(jnp.float32)
        to[2 * RIM:EDGE_ROWS, :] = jnp.broadcast_to(row, (8, NJ))
        corners = jnp.concatenate([halo[0:RIM, near, :], spare], 0)
        to[EDGE_ROWS:MESSAGE, :] = lax.dot_general(
            picks(), corners, (((1,), (1,)), ((), ())), precision=EXACT, preferred_element_type=jnp.float32
        )


def levels(x, edge):
    k = iota(x.shape, 0)
    above = jnp.where(k == NZ - 1, x if edge else 0.0, pltpu.roll(x, NZ - 1, 0))
    below = jnp.where(k == 0, x if edge else 0.0, pltpu.roll(x, 1, 0))
    return above, below


def row_rates(near, far, height, sign):
    u, v, w = near[0], near[1], near[2]
    k_cell = near[NF]
    k_above, k_below = levels(k_cell, True)
    drag = jnp.where(iota(u.shape, 0).astype(jnp.float32) < height, DRAG_COEF, 0.0)
    resist = drag * jnp.sqrt(u * u + v * v + w * w + SPEED_EPS)
    rates = []
    for m in range(NF):
        f = near[m]
        above, below = levels(f, False)
        rate = 0.5 * (
            (k_cell + far[NF]) * (far[m] - f)
            + (k_cell + k_above) * (above - f)
            + (k_cell + k_below) * (below - f)
            + sign * u * far[m]
            - w * (above - below)
        )
        if m < 3:
            rate = rate - resist * f
        if m == 2:
            rate = rate + BUOYANCY * near[3]
        rates.append(rate)
    return rates


def split_rim(rim):
    near = [rim[a * NZ:(a + 1) * NZ, :] for a in range(NA)]
    far = [rim[RIM + a * NZ:RIM + (a + 1) * NZ, :] for a in range(NA)]
    return near, far, rim[2 * RIM:2 * RIM + 1, :]


def packet_kernel(fields_hbm, diff_hbm, heights_hbm, out, fields, diff, heights, sems):
    late = is_last()
    half = pl.ds(pl.multiple_of(jnp.where(late, NI - 8, 0), 8), 8)
    copies = [
        pltpu.make_async_copy(fields_hbm.at[:, :, half, :], fields, sems.at[0]),
        pltpu.make_async_copy(diff_hbm.at[:, half, :], diff, sems.at[1]),
        pltpu.make_async_copy(heights_hbm.at[half, :], heights, sems.at[2]),
    ]
    for copy in copies:
        copy.start()
    out[...] = jnp.zeros_like(out)
    for copy in copies:
        copy.wait()

    def row(r):
        both = [fields[m, :, r, :] for m in range(NF)], [fields[m, :, 7 - r, :] for m in range(NF)]
        parts = [jnp.where(late, b, a) for a, b in zip(*both)]
        return parts + [jnp.where(late, diff[:, 7 - r, :], diff[:, r, :])]

    near, far = row(0), row(1)
    height = jnp.where(late, heights[7:8, :], heights[0:1, :]).astype(jnp.float32)
    sign = jnp.where(late, 1.0, -1.0).astype(jnp.float32)
    rates = row_rates(near, far, height, sign)
    zero = jnp.zeros((NZ, NJ), jnp.float32)
    lower = [near[0], near[1], near[2], near[NF], rates[0], rates[1], rates[2], zero]
    upper = [near[3], near[4], near[1], near[NF], rates[3], rates[4], zero, zero]
    at = jnp.where(late, 2 * NZ, 0)
    for row in range(8):
        out[pl.ds(at, NZ), row, :] = lower[row]
        out[pl.ds(at + NZ, NZ), row, :] = upper[row]


def inverse_kernel(wrap, out):
    @pl.when(is_last())
    def _():
        total = jnp.zeros((64, NJ), jnp.float32)
        lane = iota((32, NJ), 1).astype(jnp.float32)
        for s in range(32):
            p = wrap[s:s + 1, :]
            hit = jnp.where(iota((32, NJ), 0) == p // NJ, 1.0, 0.0)
            low = jnp.where(iota((NJ, NJ), 0) == lax.rem(p, NJ), 1.0, 0.0).astype(jnp.bfloat16)
            left = jnp.concatenate([hit * lane, hit * float(s)], 0).astype(jnp.bfloat16)
            total = total + lax.dot_general(
                left, low, (((1,), (1,)), ((), ())), preferred_element_type=jnp.float32
            )
        out[...] = (total[0:32, :] + NJ * total[32:64, :]).astype(jnp.int32)


def permute_kernel(rows, wrap, inverse, out, left_side, right_side):
    first, gx, half = is_first(), lax.axis_index("gx"), lax.axis_size("gx") // 2
    target = jnp.where(first, wrap[...], inverse[...])
    column = iota(target.shape, 0) * NJ + iota(target.shape, 1)
    target = jnp.where((gx == half) | (gx == half - 1), column, target)
    upper = lax.axis_index("gy") < LEAD
    x = rows[pl.ds(jnp.where(first, 0, 32), 32)]
    x = jnp.concatenate([x[32 - LEAD:], x[:32 - LEAD]], 0)
    lane, sub = iota(x.shape, 2), iota(x.shape, 1)

    def after(y):
        return jnp.concatenate([y[1:], y[:1]], 0)

    def before(y):
        return jnp.concatenate([y[-1:], y[:-1]], 0)

    left, right = pltpu.roll(x, NJ - 1, 2), pltpu.roll(x, 1, 2)
    north = jnp.where(lane == NJ - 1, after(left), left)
    south = jnp.where(lane == 0, before(right), right)
    v = jnp.where(upper, x[:, 2:3, :], x[:, 1:2, :])
    k_cell, k_north, k_south = x[:, 3:4, :], north[:, 3:4, :], south[:, 3:4, :]
    term = 0.5 * (
        (k_cell + k_north) * (north - x) + (k_cell + k_south) * (south - x) - v * (north - south)
    )
    x = x + jnp.where((sub >= 4) & (sub < 7), pltpu.roll(term, 4, 1), 0.0)

    part_a = x.astype(jnp.bfloat16).astype(jnp.float32)
    rest = x - part_a
    part_b = rest.astype(jnp.bfloat16).astype(jnp.float32)
    part_c = rest - part_b
    for s in range(32):
        t = target[s:s + 1, :]
        hi, lo = lax.shift_right_logical(t, 8), lax.bitwise_and(t, 255)
        stack = jnp.concatenate([part_a[s], part_b[s], part_c[s]], 0)
        masked = jnp.concatenate([jnp.where(hi == h, stack, 0.0) for h in range(16)], 0)
        at = slice(s * NJ, (s + 1) * NJ)
        left_side[:, at] = masked.astype(jnp.bfloat16)
        right_side[:, at] = jnp.where(iota((256, NJ), 0) == lo, 1.0, 0.0).astype(jnp.bfloat16)
    moved = lax.dot_general(
        left_side[...], right_side[...], (((1,), (1,)), ((), ())), preferred_element_type=jnp.float32
    )
    for h in range(16):
        at = h * 24
        tile = moved[at:at + 8, :] + moved[at + 8:at + 16, :] + moved[at + 16:at + 24, :]
        out[2 * h] = tile[:, 0:NJ]
        out[2 * h + 1] = tile[:, NJ:2 * NJ]
    y = out[...]
    prior, later = before(y), after(y)
    last = jnp.zeros_like(y)
    for r in range(4):
        corner = jnp.where(lane < 64, pltpu.roll(later, r, 2), pltpu.roll(prior, (NJ - r) % NJ, 2))
        corner = pltpu.roll(corner, 7 - r, 1)
        last = jnp.where((lane == r) | (lane == NJ - 1 - r), corner, last)
    y = jnp.where(sub == 7, last, y)
    out[...] = y


def beside(m, h):
    lane = iota(m.shape, 1)
    m_left, h_left = pltpu.roll(m, NJ - 1, 1), pltpu.roll(h, NJ - 1, 1)
    m_right, h_right = pltpu.roll(m, 1, 1), pltpu.roll(h, 1, 1)
    at_end, at_start = lane == NJ - 1, lane == 0
    return (
        jnp.where(at_end, h_left, m_left),
        jnp.where(at_start, h_right, m_right),
        jnp.where(at_end, m_left, h_left),
        jnp.where(at_start, m_right, h_right),
    )


def rates_of(cells, k_cell, k_sides, drag, sign=None):
    u, v, w = cells[0][0], cells[1][0], cells[2][0]
    resist = drag * jnp.sqrt(u * u + v * v + w * w + SPEED_EPS)
    if sign is not None:
        u = sign * u
    sums = [k_cell + side for side in k_sides]
    total = sums[0] + sums[1] + sums[2] + sums[3] + sums[4] + sums[5]
    rates = []
    for m in range(NF):
        f, e, ws, n, s, up, dn = cells[m]
        rate = 0.5 * (
            (sums[0] - u) * e + (sums[1] + u) * ws
            + (sums[2] - v) * n + (sums[3] + v) * s
            + (sums[4] - w) * up + (sums[5] + w) * dn
            - total * f
        )
        if m < 3:
            rate = rate - resist * f
        if m == 2:
            rate = rate + BUOYANCY * cells[3][0]
        rates.append(rate)
    return rates


def sections_kernel(fields, diff, heights, halo, out, kept, one, one_halo):
    sub = iota((NI, NJ), 0)

    def along(x):
        return (
            jnp.where(sub == NI - 1, 0.0, pltpu.roll(x, NI - 1, 0)),
            jnp.where(sub == 0, 0.0, pltpu.roll(x, 1, 0)),
        )

    high_main = heights[...].astype(jnp.float32)
    high_halo = halo[HALO - 1]

    def section_one(k, _):
        up, dn = jnp.minimum(k + 1, NZ - 1), jnp.maximum(k - 1, 0)
        has_up = jnp.where(k < NZ - 1, 1.0, 0.0).astype(jnp.float32)
        has_dn = jnp.where(k > 0, 1.0, 0.0).astype(jnp.float32)
        level = k.astype(jnp.float32)
        k_main, k_halo = diff[k], halo[NF * NZ + k]
        n, s, hn, hs = beside(k_main, k_halo)
        k_sides = (*along(k_main), n, s, diff[up], diff[dn])
        kh_sides = (*along(k_halo), hn, hs, halo[NF * NZ + up], halo[NF * NZ + dn])
        cells, halos = [], []
        for m in range(NF):
            f, h = fields[m, k], halo[m * NZ + k]
            n, s, hn, hs = beside(f, h)
            cells.append((f, *along(f), n, s, has_up * fields[m, up], has_dn * fields[m, dn]))
            halos.append((h, *along(h), hn, hs, has_up * halo[m * NZ + up], has_dn * halo[m * NZ + dn]))
        drag = jnp.where(level < high_main, DRAG_COEF, 0.0)
        drag_h = jnp.where(level < high_halo, DRAG_COEF, 0.0)
        rates = rates_of(cells, k_main, k_sides, drag)
        rates_h = rates_of(halos, k_halo, kh_sides, drag_h)
        for m in range(NF):
            one[m, k] = cells[m][0] + TIME_STEP / 3.0 * rates[m]
            one_halo[m, k] = halos[m][0] + TIME_STEP / 3.0 * rates_h[m]
        return 0

    lax.fori_loop(0, NZ, section_one, 0)

    def section_two(k, _):
        up, dn = jnp.minimum(k + 1, NZ - 1), jnp.maximum(k - 1, 0)
        has_up = jnp.where(k < NZ - 1, 1.0, 0.0).astype(jnp.float32)
        has_dn = jnp.where(k > 0, 1.0, 0.0).astype(jnp.float32)
        k_main = diff[k]
        n, s, _, _ = beside(k_main, halo[NF * NZ + k])
        k_sides = (*along(k_main), n, s, diff[up], diff[dn])
        cells = []
        for m in range(NF):
            f = one[m, k]
            n, s, _, _ = beside(f, one_halo[m, k])
            cells.append((f, *along(f), n, s, has_up * one[m, up], has_dn * one[m, dn]))
        drag = jnp.where(k.astype(jnp.float32) < high_main, DRAG_COEF, 0.0)
        rates = rates_of(cells, k_main, k_sides, drag)
        for m in range(NF):
            out[m, k] = fields[m, k] + TIME_STEP / 2.0 * rates[m]
        return 0

    lax.fori_loop(0, NZ, section_two, 0)
    for m in range(NF):
        for r in range(3):
            kept[0, m, r] = one[m, :, r, :]
            kept[1, m, r] = one[m, :, NI - 1 - r, :]
        for r in range(2):
            kept[0, m, 3 + r] = one_halo[m, :, r, :]
            kept[1, m, 3 + r] = one_halo[m, :, NI - 1 - r, :]


def redo_side(side, outer, corner, rates, fields, diff, heights, halo, kept, out):
    sign = 1.0 if side == 0 else -1.0
    rows = [r if side == 0 else NI - 1 - r for r in range(3)]

    def block_row(i, r):
        return (diff if i == NF else fields.at[i])[:, rows[r], :]

    def halo_row(i, r):
        return halo[i * NZ:(i + 1) * NZ, rows[r], :]

    own = [block_row(i, 0) for i in range(NA)]
    beyond = [halo_row(i, 0) for i in range(NA)]
    ones, one_halos = [], []
    for m in range(NF):
        rate = rates[m] + 0.5 * (
            (outer[NF] + own[NF]) * (own[m] - outer[m]) - sign * outer[0] * own[m]
        )
        one_out = outer[m] + TIME_STEP / 3.0 * rate
        rate = (own[NF] + outer[NF] + sign * own[0]) * outer[m] - outer[NF] * own[m]
        one_own = kept[side, m, 0] + TIME_STEP / 6.0 * rate
        rate = (beyond[NF] + corner[NF] + sign * beyond[0]) * corner[m] - corner[NF] * beyond[m]
        ones.append([one_out, one_own, kept[side, m, 1], kept[side, m, 2]])
        one_halos.append([kept[side, m, 3] + TIME_STEP / 6.0 * rate, kept[side, m, 4]])
    k_rows = [outer[NF], own[NF], block_row(NF, 1), block_row(NF, 2)]
    k_halos = [beyond[NF], halo_row(NF, 1)]
    for r in range(2):
        k_cell = k_rows[r + 1]
        k_n, k_s, _, _ = beside(k_cell, k_halos[r])
        k_sides = (k_rows[r + 2], k_rows[r], k_n, k_s, *levels(k_cell, True))
        cells = []
        for m in range(NF):
            f = ones[m][r + 1]
            n, s, _, _ = beside(f, one_halos[m][r])
            cells.append((f, ones[m][r + 2], ones[m][r], n, s, *levels(f, False)))
        drag = jnp.where(iota((NZ, NJ), 0) < heights[rows[r]:rows[r] + 1, :], DRAG_COEF, 0.0)
        rates = rates_of(cells, k_cell, k_sides, drag, sign)
        for m in range(NF):
            out[m, :, rows[r], :] = block_row(m, r) + TIME_STEP / 2.0 * rates[m]


def edges_kernel(fields, diff, heights, halo, kept, west, east, done, out):
    out[...] = done[...]
    for side, rim, beyond_wrap, sign in ((0, west, is_first(), 1.0), (1, east, is_last(), -1.0)):
        @pl.when(jnp.logical_not(beyond_wrap))
        def _(side=side, rim=rim, sign=sign):
            outer, far, height = split_rim(rim)
            rates = row_rates(outer, far, height, sign)
            corner = lax.dot_general(
                rim[EDGE_ROWS:MESSAGE, :], picks(), (((0,), (0,)), ((), ())),
                precision=EXACT, preferred_element_type=jnp.float32,
            )
            corner = [corner[i * NZ:(i + 1) * NZ, :] for i in range(NA)]
            sides = [beside(outer[i], corner[i]) for i in range(NA)]
            k_cell, k_n, k_s = outer[NF], sides[NF][0], sides[NF][1]
            for m in range(NF):
                f, n, s = outer[m], sides[m][0], sides[m][1]
                rates[m] = rates[m] + 0.5 * (
                    (k_cell + k_n) * (n - f) + (k_cell + k_s) * (s - f) - outer[1] * (n - s)
                )
            redo_side(side, outer, corner, rates, fields, diff, heights, halo, kept, out)


def wrap_kernel(fields, diff, heights, halo, kept, wrapped, done, out):
    out[...] = done[...]
    lane = iota((NZ, NJ), 1)
    place = {0: (LEAD, 0), 1: (LEAD, 1), 2: (LEAD, 2), NF: (LEAD, 3), 3: (0, 0), 4: (0, 1)}
    for side, mine in ((0, is_first()), (1, is_last())):
        @pl.when(mine)
        def _(side=side):
            rates, outer, corner = [], [], []
            for m in range(NF):
                half, row = (LEAD, 4 + m) if m < 3 else (0, 1 + m)
                rates.append(wrapped[half:half + NZ, row, :])
            for i in range(NA):
                half, row = place[i]
                outer.append(wrapped[half:half + NZ, row, :])
                spare = wrapped[half:half + NZ, 7, :]
                corner.append(
                    jnp.where(lane < 64, pltpu.roll(spare, (NJ - row) % NJ, 1), pltpu.roll(spare, row, 1))
                )
            redo_side(side, outer, corner, rates, fields, diff, heights, halo, kept, out)


def shards(fields, diffusivity, heights, wrap_map):
    count_x, count_y = lax.axis_size("gx"), lax.axis_size("gy")
    last = count_x - 1
    pack = f32(2, PACK)
    block = (fields, diffusivity, heights)
    half = pltpu.VMEM((NF, NZ, 8, NJ), jnp.float32), pltpu.VMEM((NZ, 8, NJ), jnp.float32)
    packets = pl.pallas_call(
        packet_kernel,
        out_shape=f32(2 * count_y, 8, NJ),
        in_specs=[pl.BlockSpec(memory_space=pl.ANY)] * 3,
        out_specs=VMEM,
        scratch_shapes=[*half, pltpu.VMEM((8, NJ), jnp.int32), pltpu.SemaphoreType.DMA((3,))],
        compiler_params=pltpu.CompilerParams(vmem_limit_bytes=56 * 1024 * 1024),
        name="packets",
    )(*block)

    half_x = count_x // 2
    row_pairs = [(0, last), (half_x, half_x - 1)] + [(i, i + half_x) for i in range(1, half_x - 1)]
    def line(*rows):
        return [r * count_y + (i + LEAD) % count_y for r in rows for i in range(count_y)]

    groups = [line(b, a) for a, b in row_pairs]
    rows = lax.all_to_all(packets, ("gx", "gy"), 0, 0, axis_index_groups=groups)

    low = [(i, i + 1) for i in range(0, count_y, 2)]
    high = [(i, (i + 1) % count_y) for i in range(1, count_y, 2)]
    tied = lax.optimization_barrier((*block, packets))[:3]
    to_a, to_b = call(pack_kernel, (pack, pack), *tied, name="pack")
    from_b = lax.ppermute(to_b, "gy", high + [(j, i) for i, j in high])
    from_a = lax.ppermute(to_a, "gy", low + [(j, i) for i, j in low])

    wrap = wrap_map.reshape(count_y, NJ)
    inverse = call(
        inverse_kernel, jax.ShapeDtypeStruct((count_y, NJ), jnp.int32), wrap, name="inverse"
    )
    rows, inverse, from_a = lax.optimization_barrier((rows, inverse, from_a))
    moved = call(
        permute_kernel, f32(count_y, 8, NJ), rows, wrap, inverse, name="permute",
        scratch=[pltpu.VMEM((384, 32 * NJ), jnp.bfloat16), pltpu.VMEM((256, 32 * NJ), jnp.bfloat16)],
    )
    moved, from_b = lax.optimization_barrier((moved, from_b))
    wrapped = lax.all_to_all(moved, "gy", 0, 0)

    message = f32(MESSAGE, NJ)
    halo, to_east, to_west = call(
        unpack_kernel, (f32(HALO, NI, NJ), message, message),
        from_a, from_b, *block, name="unpack",
            )
    east_pairs = [(i, i + 1) for i in range(last) if i + 1 != half_x]
    west = lax.ppermute(to_east, "gx", east_pairs)
    east = lax.ppermute(to_west, "gx", [(j, i) for i, j in east_pairs])

    state = pltpu.VMEM((NF, NZ, NI, NJ), jnp.float32)
    done, kept = call(
        sections_kernel, (f32(NF, NZ, NI, NJ), f32(2, NF, 5, NZ, NJ)),
        *block, halo, name="sections", scratch=[state, state],
    )
    done = call(
        edges_kernel, f32(NF, NZ, NI, NJ), *block, halo, kept, west, east, done, name="edges"
    )
    return call(
        wrap_kernel, f32(NF, NZ, NI, NJ), *block, halo, kept, wrapped, done, name="wrapped_rows"
    )


def solution(mesh):
    in_specs = (P(None, None, "gx", "gy"), P(None, "gx", "gy"), P("gx", "gy"), P())
    out_specs = P(None, None, "gx", "gy")
    return jax.shard_map(shards, mesh=mesh, in_specs=in_specs, out_specs=out_specs, check_vma=False)
```

```python
import jax
import jax.numpy as jnp
from jax import lax
from jax.experimental import pallas as pl
from jax.experimental.pallas import tpu as pltpu
from jax.sharding import PartitionSpec as P

DRAG_COEF = 1.0
TIME_STEP = 0.3
BUOYANCY = 0.5
SPEED_EPS = 0.01

NF = 5
NA = 6
NZ = 16
NI = 16
NJ = 128
RIM = NA * NZ
EDGE_ROWS = 2 * RIM + 8
MESSAGE = EDGE_ROWS + 8
BLOCK = NA * NZ * NI
PACK = BLOCK + 128
HEIGHT_AT = BLOCK
HALO = RIM + 1

LEAD = 20

VMEM = pl.BlockSpec(memory_space=pltpu.VMEM)
EXACT = lax.Precision.HIGHEST


def iota(shape, dim):
    return lax.broadcasted_iota(jnp.int32, shape, dim)


def call(kernel, outs, *args, scratch=(), name=None):
    return pl.pallas_call(
        kernel,
        out_shape=outs,
        in_specs=[VMEM] * len(args),
        out_specs=jax.tree.map(lambda _: VMEM, outs),
        scratch_shapes=list(scratch),
        compiler_params=pltpu.CompilerParams(vmem_limit_bytes=40 * 1024 * 1024),
        name=name,
    )(*args)


def f32(*shape):
    return jax.ShapeDtypeStruct(shape, jnp.float32)


def picks():
    row, lane = iota((8, NJ), 0), iota((8, NJ), 1)
    want = jnp.where(row < 2, row, jnp.where(row < 4, NJ - 4 + row, -1))
    return jnp.where(lane == want, 1.0, 0.0).astype(jnp.float32)


def is_first():
    return lax.rem(lax.axis_index("gx"), lax.axis_size("gx") // 2) == 0


def is_last():
    half = lax.axis_size("gx") // 2
    return lax.rem(lax.axis_index("gx"), half) == half - 1


def spread_out(cols):
    part_a = cols.astype(jnp.bfloat16).astype(jnp.float32)
    rest = cols - part_a
    part_b = rest.astype(jnp.bfloat16).astype(jnp.float32)
    parts = jnp.concatenate([part_a, part_b, rest - part_b, jnp.zeros_like(cols)], 0)
    hot = jnp.concatenate([picks()] * 4, 0)
    return lax.dot_general(
        parts.astype(jnp.bfloat16), hot.astype(jnp.bfloat16), (((0,), (0,)), ((), ())),
        preferred_element_type=jnp.float32,
    )


def pack_kernel(fields, diff, heights, to_a, to_b):
    even = lax.rem(lax.axis_index("gy"), 2) == 0
    rows = jnp.concatenate(
        [
            fields[...].reshape(NF * NZ * NI, NJ),
            diff[...].reshape(NZ * NI, NJ),
            heights[...].astype(jnp.float32),
            jnp.zeros((PACK - HEIGHT_AT - NI, NJ), jnp.float32),
        ],
        0,
    )
    cols = lax.dot_general(
        picks(), rows, (((1,), (1,)), ((), ())), precision=EXACT, preferred_element_type=jnp.float32
    )
    low, high = cols[0:2, :], cols[2:4, :]
    to_a[...] = jnp.where(even, high, low)
    to_b[...] = jnp.where(even, low, high)


def unpack_kernel(from_a, from_b, fields, diff, heights, halo, to_east, to_west):
    even = lax.rem(lax.axis_index("gy"), 2) == 0
    a, b = from_a[...], from_b[...]
    north, south = jnp.where(even, a, b), jnp.where(even, b, a)
    cols = jnp.concatenate([north, south, jnp.zeros((4, PACK), jnp.float32)], 0)
    spread = spread_out(cols)
    halo[...] = spread[0:HALO * NI, :].reshape(HALO, NI, NJ)
    spare = jnp.zeros((NJ - RIM, NJ), jnp.float32)
    for to, near, far in ((to_east, NI - 1, NI - 2), (to_west, 0, 1)):
        for i in range(NA):
            src = diff if i == NF else fields.at[i]
            to[i * NZ:(i + 1) * NZ, :] = src[:, near, :]
            to[RIM + i * NZ:RIM + (i + 1) * NZ, :] = src[:, far, :]
        row = heights[near:near + 1, :].astype(jnp.float32)
        to[2 * RIM:EDGE_ROWS, :] = jnp.broadcast_to(row, (8, NJ))
        corners = jnp.concatenate([halo[0:RIM, near, :], spare], 0)
        to[EDGE_ROWS:MESSAGE, :] = lax.dot_general(
            picks(), corners, (((1,), (1,)), ((), ())), precision=EXACT, preferred_element_type=jnp.float32
        )


def levels(x, edge):
    k = iota(x.shape, 0)
    above = jnp.where(k == NZ - 1, x if edge else 0.0, pltpu.roll(x, NZ - 1, 0))
    below = jnp.where(k == 0, x if edge else 0.0, pltpu.roll(x, 1, 0))
    return above, below


def row_rates(near, far, height, sign):
    u, v, w = near[0], near[1], near[2]
    k_cell = near[NF]
    k_above, k_below = levels(k_cell, True)
    drag = jnp.where(iota(u.shape, 0).astype(jnp.float32) < height, DRAG_COEF, 0.0)
    resist = drag * jnp.sqrt(u * u + v * v + w * w + SPEED_EPS)
    rates = []
    for m in range(NF):
        f = near[m]
        above, below = levels(f, False)
        rate = 0.5 * (
            (k_cell + far[NF]) * (far[m] - f)
            + (k_cell + k_above) * (above - f)
            + (k_cell + k_below) * (below - f)
            + sign * u * far[m]
            - w * (above - below)
        )
        if m < 3:
            rate = rate - resist * f
        if m == 2:
            rate = rate + BUOYANCY * near[3]
        rates.append(rate)
    return rates


def split_rim(rim):
    near = [rim[a * NZ:(a + 1) * NZ, :] for a in range(NA)]
    far = [rim[RIM + a * NZ:RIM + (a + 1) * NZ, :] for a in range(NA)]
    return near, far, rim[2 * RIM:2 * RIM + 1, :]


def packet_kernel(fields_hbm, diff_hbm, heights_hbm, out, fields, diff, heights, sems):
    late = is_last()
    half = pl.ds(pl.multiple_of(jnp.where(late, NI - 8, 0), 8), 8)
    copies = [
        pltpu.make_async_copy(fields_hbm.at[:, :, half, :], fields, sems.at[0]),
        pltpu.make_async_copy(diff_hbm.at[:, half, :], diff, sems.at[1]),
        pltpu.make_async_copy(heights_hbm.at[half, :], heights, sems.at[2]),
    ]
    for copy in copies:
        copy.start()
    out[...] = jnp.zeros_like(out)
    for copy in copies:
        copy.wait()

    def row(r):
        both = [fields[m, :, r, :] for m in range(NF)], [fields[m, :, 7 - r, :] for m in range(NF)]
        parts = [jnp.where(late, b, a) for a, b in zip(*both)]
        return parts + [jnp.where(late, diff[:, 7 - r, :], diff[:, r, :])]

    near, far = row(0), row(1)
    height = jnp.where(late, heights[7:8, :], heights[0:1, :]).astype(jnp.float32)
    sign = jnp.where(late, 1.0, -1.0).astype(jnp.float32)
    rates = row_rates(near, far, height, sign)
    zero = jnp.zeros((NZ, NJ), jnp.float32)
    lower = [near[0], near[1], near[2], near[NF], rates[0], rates[1], rates[2], zero]
    upper = [near[3], near[4], near[1], near[NF], rates[3], rates[4], zero, zero]
    at = jnp.where(late, 2 * NZ, 0)
    for row in range(8):
        out[pl.ds(at, NZ), row, :] = lower[row]
        out[pl.ds(at + NZ, NZ), row, :] = upper[row]


def inverse_kernel(wrap, out):
    @pl.when(is_last())
    def _():
        total = jnp.zeros((64, NJ), jnp.float32)
        lane = iota((32, NJ), 1).astype(jnp.float32)
        for s in range(32):
            p = wrap[s:s + 1, :]
            hit = jnp.where(iota((32, NJ), 0) == p // NJ, 1.0, 0.0)
            low = jnp.where(iota((NJ, NJ), 0) == lax.rem(p, NJ), 1.0, 0.0).astype(jnp.bfloat16)
            left = jnp.concatenate([hit * lane, hit * float(s)], 0).astype(jnp.bfloat16)
            total = total + lax.dot_general(
                left, low, (((1,), (1,)), ((), ())), preferred_element_type=jnp.float32
            )
        out[...] = (total[0:32, :] + NJ * total[32:64, :]).astype(jnp.int32)


def permute_kernel(rows, wrap, inverse, out, left_side, right_side):
    first, gx, half = is_first(), lax.axis_index("gx"), lax.axis_size("gx") // 2
    target = jnp.where(first, wrap[...], inverse[...])
    column = iota(target.shape, 0) * NJ + iota(target.shape, 1)
    target = jnp.where((gx == half) | (gx == half - 1), column, target)
    upper = lax.rem(lax.axis_index("gy") + 32 - LEAD, 32) >= NZ
    x = rows[pl.ds(jnp.where(first, 0, 32), 32)]
    x = jnp.concatenate([x[32 - LEAD:], x[:32 - LEAD]], 0)
    lane, sub = iota(x.shape, 2), iota(x.shape, 1)

    def after(y):
        return jnp.concatenate([y[1:], y[:1]], 0)

    def before(y):
        return jnp.concatenate([y[-1:], y[:-1]], 0)

    left, right = pltpu.roll(x, NJ - 1, 2), pltpu.roll(x, 1, 2)
    north = jnp.where(lane == NJ - 1, after(left), left)
    south = jnp.where(lane == 0, before(right), right)
    v = jnp.where(upper, x[:, 2:3, :], x[:, 1:2, :])
    k_cell, k_north, k_south = x[:, 3:4, :], north[:, 3:4, :], south[:, 3:4, :]
    term = 0.5 * (
        (k_cell + k_north) * (north - x) + (k_cell + k_south) * (south - x) - v * (north - south)
    )
    x = x + jnp.where((sub >= 4) & (sub < 7), pltpu.roll(term, 4, 1), 0.0)

    part_a = x.astype(jnp.bfloat16).astype(jnp.float32)
    rest = x - part_a
    part_b = rest.astype(jnp.bfloat16).astype(jnp.float32)
    part_c = rest - part_b
    for s in range(32):
        t = target[s:s + 1, :]
        hi, lo = lax.shift_right_logical(t, 8), lax.bitwise_and(t, 255)
        stack = jnp.concatenate([part_a[s], part_b[s], part_c[s]], 0)
        masked = jnp.concatenate([jnp.where(hi == h, stack, 0.0) for h in range(16)], 0)
        at = slice(s * NJ, (s + 1) * NJ)
        left_side[:, at] = masked.astype(jnp.bfloat16)
        right_side[:, at] = jnp.where(iota((256, NJ), 0) == lo, 1.0, 0.0).astype(jnp.bfloat16)
    moved = lax.dot_general(
        left_side[...], right_side[...], (((1,), (1,)), ((), ())), preferred_element_type=jnp.float32
    )
    for h in range(16):
        at = h * 24
        tile = moved[at:at + 8, :] + moved[at + 8:at + 16, :] + moved[at + 16:at + 24, :]
        out[2 * h] = tile[:, 0:NJ]
        out[2 * h + 1] = tile[:, NJ:2 * NJ]
    y = out[...]
    prior, later = before(y), after(y)
    last = jnp.zeros_like(y)
    for r in range(4):
        corner = jnp.where(lane < 64, pltpu.roll(later, r, 2), pltpu.roll(prior, (NJ - r) % NJ, 2))
        corner = pltpu.roll(corner, 7 - r, 1)
        last = jnp.where((lane == r) | (lane == NJ - 1 - r), corner, last)
    y = jnp.where(sub == 7, last, y)
    out[...] = jnp.concatenate([y[LEAD:], y[:LEAD]], 0)


def beside(m, h):
    lane = iota(m.shape, 1)
    m_left, h_left = pltpu.roll(m, NJ - 1, 1), pltpu.roll(h, NJ - 1, 1)
    m_right, h_right = pltpu.roll(m, 1, 1), pltpu.roll(h, 1, 1)
    at_end, at_start = lane == NJ - 1, lane == 0
    return (
        jnp.where(at_end, h_left, m_left),
        jnp.where(at_start, h_right, m_right),
        jnp.where(at_end, m_left, h_left),
        jnp.where(at_start, m_right, h_right),
    )


def rates_of(cells, k_cell, k_sides, drag, sign=None):
    u, v, w = cells[0][0], cells[1][0], cells[2][0]
    resist = drag * jnp.sqrt(u * u + v * v + w * w + SPEED_EPS)
    if sign is not None:
        u = sign * u
    sums = [k_cell + side for side in k_sides]
    total = sums[0] + sums[1] + sums[2] + sums[3] + sums[4] + sums[5]
    rates = []
    for m in range(NF):
        f, e, ws, n, s, up, dn = cells[m]
        rate = 0.5 * (
            (sums[0] - u) * e + (sums[1] + u) * ws
            + (sums[2] - v) * n + (sums[3] + v) * s
            + (sums[4] - w) * up + (sums[5] + w) * dn
            - total * f
        )
        if m < 3:
            rate = rate - resist * f
        if m == 2:
            rate = rate + BUOYANCY * cells[3][0]
        rates.append(rate)
    return rates


def sections_kernel(fields, diff, heights, halo, out, kept, one, one_halo):
    sub = iota((NI, NJ), 0)

    def along(x):
        return (
            jnp.where(sub == NI - 1, 0.0, pltpu.roll(x, NI - 1, 0)),
            jnp.where(sub == 0, 0.0, pltpu.roll(x, 1, 0)),
        )

    high_main = heights[...].astype(jnp.float32)
    high_halo = halo[HALO - 1]

    def section_one(k, _):
        up, dn = jnp.minimum(k + 1, NZ - 1), jnp.maximum(k - 1, 0)
        has_up = jnp.where(k < NZ - 1, 1.0, 0.0).astype(jnp.float32)
        has_dn = jnp.where(k > 0, 1.0, 0.0).astype(jnp.float32)
        level = k.astype(jnp.float32)
        k_main, k_halo = diff[k], halo[NF * NZ + k]
        n, s, hn, hs = beside(k_main, k_halo)
        k_sides = (*along(k_main), n, s, diff[up], diff[dn])
        kh_sides = (*along(k_halo), hn, hs, halo[NF * NZ + up], halo[NF * NZ + dn])
        cells, halos = [], []
        for m in range(NF):
            f, h = fields[m, k], halo[m * NZ + k]
            n, s, hn, hs = beside(f, h)
            cells.append((f, *along(f), n, s, has_up * fields[m, up], has_dn * fields[m, dn]))
            halos.append((h, *along(h), hn, hs, has_up * halo[m * NZ + up], has_dn * halo[m * NZ + dn]))
        drag = jnp.where(level < high_main, DRAG_COEF, 0.0)
        drag_h = jnp.where(level < high_halo, DRAG_COEF, 0.0)
        rates = rates_of(cells, k_main, k_sides, drag)
        rates_h = rates_of(halos, k_halo, kh_sides, drag_h)
        for m in range(NF):
            one[m, k] = cells[m][0] + TIME_STEP / 3.0 * rates[m]
            one_halo[m, k] = halos[m][0] + TIME_STEP / 3.0 * rates_h[m]
        return 0

    lax.fori_loop(0, NZ, section_one, 0, unroll=4)

    def section_two(k, _):
        up, dn = jnp.minimum(k + 1, NZ - 1), jnp.maximum(k - 1, 0)
        has_up = jnp.where(k < NZ - 1, 1.0, 0.0).astype(jnp.float32)
        has_dn = jnp.where(k > 0, 1.0, 0.0).astype(jnp.float32)
        k_main = diff[k]
        n, s, _, _ = beside(k_main, halo[NF * NZ + k])
        k_sides = (*along(k_main), n, s, diff[up], diff[dn])
        cells = []
        for m in range(NF):
            f = one[m, k]
            n, s, _, _ = beside(f, one_halo[m, k])
            cells.append((f, *along(f), n, s, has_up * one[m, up], has_dn * one[m, dn]))
        drag = jnp.where(k.astype(jnp.float32) < high_main, DRAG_COEF, 0.0)
        rates = rates_of(cells, k_main, k_sides, drag)
        for m in range(NF):
            out[m, k] = fields[m, k] + TIME_STEP / 2.0 * rates[m]
        return 0

    lax.fori_loop(0, NZ, section_two, 0, unroll=4)
    for m in range(NF):
        for r in range(3):
            kept[0, m, r] = one[m, :, r, :]
            kept[1, m, r] = one[m, :, NI - 1 - r, :]
        for r in range(2):
            kept[0, m, 3 + r] = one_halo[m, :, r, :]
            kept[1, m, 3 + r] = one_halo[m, :, NI - 1 - r, :]


def redo_side(side, outer, corner, rates, fields, diff, heights, halo, kept, out):
    sign = 1.0 if side == 0 else -1.0
    rows = [r if side == 0 else NI - 1 - r for r in range(3)]

    def block_row(i, r):
        return (diff if i == NF else fields.at[i])[:, rows[r], :]

    def halo_row(i, r):
        return halo[i * NZ:(i + 1) * NZ, rows[r], :]

    own = [block_row(i, 0) for i in range(NA)]
    beyond = [halo_row(i, 0) for i in range(NA)]
    ones, one_halos = [], []
    for m in range(NF):
        rate = rates[m] + 0.5 * (
            (outer[NF] + own[NF]) * (own[m] - outer[m]) - sign * outer[0] * own[m]
        )
        one_out = outer[m] + TIME_STEP / 3.0 * rate
        rate = (own[NF] + outer[NF] + sign * own[0]) * outer[m] - outer[NF] * own[m]
        one_own = kept[side, m, 0] + TIME_STEP / 6.0 * rate
        rate = (beyond[NF] + corner[NF] + sign * beyond[0]) * corner[m] - corner[NF] * beyond[m]
        ones.append([one_out, one_own, kept[side, m, 1], kept[side, m, 2]])
        one_halos.append([kept[side, m, 3] + TIME_STEP / 6.0 * rate, kept[side, m, 4]])
    k_rows = [outer[NF], own[NF], block_row(NF, 1), block_row(NF, 2)]
    k_halos = [beyond[NF], halo_row(NF, 1)]
    for r in range(2):
        k_cell = k_rows[r + 1]
        k_n, k_s, _, _ = beside(k_cell, k_halos[r])
        k_sides = (k_rows[r + 2], k_rows[r], k_n, k_s, *levels(k_cell, True))
        cells = []
        for m in range(NF):
            f = ones[m][r + 1]
            n, s, _, _ = beside(f, one_halos[m][r])
            cells.append((f, ones[m][r + 2], ones[m][r], n, s, *levels(f, False)))
        drag = jnp.where(iota((NZ, NJ), 0) < heights[rows[r]:rows[r] + 1, :], DRAG_COEF, 0.0)
        rates = rates_of(cells, k_cell, k_sides, drag, sign)
        for m in range(NF):
            out[m, :, rows[r], :] = block_row(m, r) + TIME_STEP / 2.0 * rates[m]


def edges_kernel(fields, diff, heights, halo, kept, west, east, done, out):
    out[...] = done[...]
    for side, rim, beyond_wrap, sign in ((0, west, is_first(), 1.0), (1, east, is_last(), -1.0)):
        @pl.when(jnp.logical_not(beyond_wrap))
        def _(side=side, rim=rim, sign=sign):
            outer, far, height = split_rim(rim)
            rates = row_rates(outer, far, height, sign)
            corner = spread_out(rim[EDGE_ROWS:MESSAGE, :])
            corner = [corner[i * NZ:(i + 1) * NZ, :] for i in range(NA)]
            sides = [beside(outer[i], corner[i]) for i in range(NA)]
            k_cell, k_n, k_s = outer[NF], sides[NF][0], sides[NF][1]
            for m in range(NF):
                f, n, s = outer[m], sides[m][0], sides[m][1]
                rates[m] = rates[m] + 0.5 * (
                    (k_cell + k_n) * (n - f) + (k_cell + k_s) * (s - f) - outer[1] * (n - s)
                )
            redo_side(side, outer, corner, rates, fields, diff, heights, halo, kept, out)


def wrap_kernel(fields, diff, heights, halo, kept, wrapped, done, out):
    out[...] = done[...]
    lane = iota((NZ, NJ), 1)
    place = {0: (0, 0), 1: (0, 1), 2: (0, 2), NF: (0, 3), 3: (NZ, 0), 4: (NZ, 1)}
    for side, mine in ((0, is_first()), (1, is_last())):
        @pl.when(mine)
        def _(side=side):
            rates, outer, corner = [], [], []
            for m in range(NF):
                half, row = (0, 4 + m) if m < 3 else (NZ, 1 + m)
                rates.append(wrapped[half:half + NZ, row, :])
            for i in range(NA):
                half, row = place[i]
                outer.append(wrapped[half:half + NZ, row, :])
                spare = wrapped[half:half + NZ, 7, :]
                corner.append(
                    jnp.where(lane < 64, pltpu.roll(spare, (NJ - row) % NJ, 1), pltpu.roll(spare, row, 1))
                )
            redo_side(side, outer, corner, rates, fields, diff, heights, halo, kept, out)


def shards(fields, diffusivity, heights, wrap_map):
    count_x, count_y = lax.axis_size("gx"), lax.axis_size("gy")
    last = count_x - 1
    pack = f32(2, PACK)
    block = (fields, diffusivity, heights)
    half = pltpu.VMEM((NF, NZ, 8, NJ), jnp.float32), pltpu.VMEM((NZ, 8, NJ), jnp.float32)
    packets = pl.pallas_call(
        packet_kernel,
        out_shape=f32(2 * count_y, 8, NJ),
        in_specs=[pl.BlockSpec(memory_space=pl.ANY)] * 3,
        out_specs=VMEM,
        scratch_shapes=[*half, pltpu.VMEM((8, NJ), jnp.int32), pltpu.SemaphoreType.DMA((3,))],
        compiler_params=pltpu.CompilerParams(vmem_limit_bytes=56 * 1024 * 1024),
        name="packets",
    )(*block)

    half_x = count_x // 2
    row_pairs = [(0, last), (half_x, half_x - 1)] + [(i, i + half_x) for i in range(1, half_x - 1)]
    def line(lead, *rows):
        return [r * count_y + (i + lead) % count_y for r in rows for i in range(count_y)]

    groups = [line(LEAD, b, a) for a, b in row_pairs]
    rows = lax.all_to_all(packets, ("gx", "gy"), 0, 0, axis_index_groups=groups)

    low = [(i, i + 1) for i in range(0, count_y, 2)]
    high = [(i, (i + 1) % count_y) for i in range(1, count_y, 2)]
    tied = lax.optimization_barrier((*block, packets))[:3]
    to_a, to_b = call(pack_kernel, (pack, pack), *tied, name="pack")
    from_b = lax.ppermute(to_b, "gy", high + [(j, i) for i, j in high])
    from_a = lax.ppermute(to_a, "gy", low + [(j, i) for i, j in low])

    wrap = wrap_map.reshape(count_y, NJ)
    inverse = call(
        inverse_kernel, jax.ShapeDtypeStruct((count_y, NJ), jnp.int32), wrap, name="inverse"
    )
    rows, inverse, from_a = lax.optimization_barrier((rows, inverse, from_a))
    moved = call(
        permute_kernel, f32(count_y, 8, NJ), rows, wrap, inverse, name="permute",
        scratch=[pltpu.VMEM((384, 32 * NJ), jnp.bfloat16), pltpu.VMEM((256, 32 * NJ), jnp.bfloat16)],
    )
    moved, from_b = lax.optimization_barrier((moved, from_b))
    groups = [line(LEAD, r) for r in range(count_x)]
    wrapped = lax.all_to_all(moved, ("gx", "gy"), 0, 0, axis_index_groups=groups)

    message = f32(MESSAGE, NJ)
    halo, to_east, to_west = call(
        unpack_kernel, (f32(HALO, NI, NJ), message, message),
        from_a, from_b, *block, name="unpack",
            )
    east_pairs = [(i, i + 1) for i in range(last) if i + 1 != half_x]
    west = lax.ppermute(to_east, "gx", east_pairs)
    east = lax.ppermute(to_west, "gx", [(j, i) for i, j in east_pairs])

    state = pltpu.VMEM((NF, NZ, NI, NJ), jnp.float32)
    done, kept = call(
        sections_kernel, (f32(NF, NZ, NI, NJ), f32(2, NF, 5, NZ, NJ)),
        *block, halo, name="sections", scratch=[state, state],
    )
    done = call(
        edges_kernel, f32(NF, NZ, NI, NJ), *block, halo, kept, west, east, done, name="edges"
    )
    return call(
        wrap_kernel, f32(NF, NZ, NI, NJ), *block, halo, kept, wrapped, done, name="wrapped_rows"
    )


def solution(mesh):
    in_specs = (P(None, None, "gx", "gy"), P(None, "gx", "gy"), P("gx", "gy"), P())
    out_specs = P(None, None, "gx", "gy")
    return jax.shard_map(shards, mesh=mesh, in_specs=in_specs, out_specs=out_specs, check_vma=False)
```

```python
import jax
import jax.numpy as jnp
from jax import lax
from jax.experimental import pallas as pl
from jax.experimental.pallas import tpu as pltpu
from jax.sharding import PartitionSpec as P

DRAG_COEF = 1.0
TIME_STEP = 0.3
BUOYANCY = 0.5
SPEED_EPS = 0.01

NF = 5
NA = 6
NZ = 16
NI = 16
NJ = 128
RIM = NA * NZ
EDGE_ROWS = 2 * RIM + 8
MESSAGE = EDGE_ROWS + 8
BLOCK = NA * NZ * NI
PACK = BLOCK + 128
HEIGHT_AT = BLOCK
HALO = RIM + 1

LEAD = 20

VMEM = pl.BlockSpec(memory_space=pltpu.VMEM)
EXACT = lax.Precision.HIGHEST


def iota(shape, dim):
    return lax.broadcasted_iota(jnp.int32, shape, dim)


def call(kernel, outs, *args, scratch=(), name=None):
    return pl.pallas_call(
        kernel,
        out_shape=outs,
        in_specs=[VMEM] * len(args),
        out_specs=jax.tree.map(lambda _: VMEM, outs),
        scratch_shapes=list(scratch),
        compiler_params=pltpu.CompilerParams(vmem_limit_bytes=40 * 1024 * 1024),
        name=name,
    )(*args)


def f32(*shape):
    return jax.ShapeDtypeStruct(shape, jnp.float32)


def picks():
    row, lane = iota((8, NJ), 0), iota((8, NJ), 1)
    want = jnp.where(row < 2, row, jnp.where(row < 4, NJ - 4 + row, -1))
    return jnp.where(lane == want, 1.0, 0.0).astype(jnp.float32)


def is_first():
    return lax.rem(lax.axis_index("gx"), lax.axis_size("gx") // 2) == 0


def is_last():
    half = lax.axis_size("gx") // 2
    return lax.rem(lax.axis_index("gx"), half) == half - 1


def spread_out(cols):
    part_a = cols.astype(jnp.bfloat16).astype(jnp.float32)
    rest = cols - part_a
    part_b = rest.astype(jnp.bfloat16).astype(jnp.float32)
    parts = jnp.concatenate([part_a, part_b, rest - part_b, jnp.zeros_like(cols)], 0)
    hot = jnp.concatenate([picks()] * 4, 0)
    return lax.dot_general(
        parts.astype(jnp.bfloat16), hot.astype(jnp.bfloat16), (((0,), (0,)), ((), ())),
        preferred_element_type=jnp.float32,
    )


def pack_kernel(fields, diff, heights, to_a, to_b):
    even = lax.rem(lax.axis_index("gy"), 2) == 0
    rows = jnp.concatenate(
        [
            fields[...].reshape(NF * NZ * NI, NJ),
            diff[...].reshape(NZ * NI, NJ),
            heights[...].astype(jnp.float32),
            jnp.zeros((PACK - HEIGHT_AT - NI, NJ), jnp.float32),
        ],
        0,
    )
    cols = lax.dot_general(
        picks(), rows, (((1,), (1,)), ((), ())), precision=EXACT, preferred_element_type=jnp.float32
    )
    low, high = cols[0:2, :], cols[2:4, :]
    to_a[...] = jnp.where(even, high, low)
    to_b[...] = jnp.where(even, low, high)


def unpack_kernel(from_a, from_b, fields, diff, heights, halo, to_east, to_west):
    even = lax.rem(lax.axis_index("gy"), 2) == 0
    a, b = from_a[...], from_b[...]
    north, south = jnp.where(even, a, b), jnp.where(even, b, a)
    cols = jnp.concatenate([north, south, jnp.zeros((4, PACK), jnp.float32)], 0)
    spread = spread_out(cols)
    halo[...] = spread[0:HALO * NI, :].reshape(HALO, NI, NJ)
    spare = jnp.zeros((NJ - RIM, NJ), jnp.float32)
    for to, near, far in ((to_east, NI - 1, NI - 2), (to_west, 0, 1)):
        for i in range(NA):
            src = diff if i == NF else fields.at[i]
            to[i * NZ:(i + 1) * NZ, :] = src[:, near, :]
            to[RIM + i * NZ:RIM + (i + 1) * NZ, :] = src[:, far, :]
        row = heights[near:near + 1, :].astype(jnp.float32)
        to[2 * RIM:EDGE_ROWS, :] = jnp.broadcast_to(row, (8, NJ))
        corners = jnp.concatenate([halo[0:RIM, near, :], spare], 0)
        to[EDGE_ROWS:MESSAGE, :] = lax.dot_general(
            picks(), corners, (((1,), (1,)), ((), ())), precision=EXACT, preferred_element_type=jnp.float32
        )


def levels(x, edge):
    k = iota(x.shape, 0)
    above = jnp.where(k == NZ - 1, x if edge else 0.0, pltpu.roll(x, NZ - 1, 0))
    below = jnp.where(k == 0, x if edge else 0.0, pltpu.roll(x, 1, 0))
    return above, below


def row_rates(near, far, height, sign):
    u, v, w = near[0], near[1], near[2]
    k_cell = near[NF]
    k_above, k_below = levels(k_cell, True)
    drag = jnp.where(iota(u.shape, 0).astype(jnp.float32) < height, DRAG_COEF, 0.0)
    resist = drag * jnp.sqrt(u * u + v * v + w * w + SPEED_EPS)
    rates = []
    for m in range(NF):
        f = near[m]
        above, below = levels(f, False)
        rate = 0.5 * (
            (k_cell + far[NF]) * (far[m] - f)
            + (k_cell + k_above) * (above - f)
            + (k_cell + k_below) * (below - f)
            + sign * u * far[m]
            - w * (above - below)
        )
        if m < 3:
            rate = rate - resist * f
        if m == 2:
            rate = rate + BUOYANCY * near[3]
        rates.append(rate)
    return rates


def split_rim(rim):
    near = [rim[a * NZ:(a + 1) * NZ, :] for a in range(NA)]
    far = [rim[RIM + a * NZ:RIM + (a + 1) * NZ, :] for a in range(NA)]
    return near, far, rim[2 * RIM:2 * RIM + 1, :]


def packet_kernel(fields_hbm, diff_hbm, heights_hbm, out, fields, diff, heights, sems):
    late = is_last()
    half = pl.ds(pl.multiple_of(jnp.where(late, NI - 8, 0), 8), 8)
    copies = [
        pltpu.make_async_copy(fields_hbm.at[:, :, half, :], fields, sems.at[0]),
        pltpu.make_async_copy(diff_hbm.at[:, half, :], diff, sems.at[1]),
        pltpu.make_async_copy(heights_hbm.at[half, :], heights, sems.at[2]),
    ]
    for copy in copies:
        copy.start()
    out[...] = jnp.zeros_like(out)
    for copy in copies:
        copy.wait()

    def row(r):
        both = [fields[m, :, r, :] for m in range(NF)], [fields[m, :, 7 - r, :] for m in range(NF)]
        parts = [jnp.where(late, b, a) for a, b in zip(*both)]
        return parts + [jnp.where(late, diff[:, 7 - r, :], diff[:, r, :])]

    near, far = row(0), row(1)
    height = jnp.where(late, heights[7:8, :], heights[0:1, :]).astype(jnp.float32)
    sign = jnp.where(late, 1.0, -1.0).astype(jnp.float32)
    rates = row_rates(near, far, height, sign)
    zero = jnp.zeros((NZ, NJ), jnp.float32)
    lower = [near[0], near[1], near[2], near[NF], rates[0], rates[1], rates[2], zero]
    upper = [near[3], near[4], near[1], near[NF], rates[3], rates[4], zero, zero]
    at = jnp.where(late, 2 * NZ, 0)
    for row in range(8):
        out[pl.ds(at, NZ), row, :] = lower[row]
        out[pl.ds(at + NZ, NZ), row, :] = upper[row]


def inverse_kernel(wrap, out):
    @pl.when(is_last())
    def _():
        total = jnp.zeros((64, NJ), jnp.float32)
        lane = iota((32, NJ), 1).astype(jnp.float32)
        for s in range(32):
            p = wrap[s:s + 1, :]
            hit = jnp.where(iota((32, NJ), 0) == p // NJ, 1.0, 0.0)
            low = jnp.where(iota((NJ, NJ), 0) == lax.rem(p, NJ), 1.0, 0.0).astype(jnp.bfloat16)
            left = jnp.concatenate([hit * lane, hit * float(s)], 0).astype(jnp.bfloat16)
            total = total + lax.dot_general(
                left, low, (((1,), (1,)), ((), ())), preferred_element_type=jnp.float32
            )
        out[...] = (total[0:32, :] + NJ * total[32:64, :]).astype(jnp.int32)


def permute_kernel(rows, wrap, inverse, out, left_side, right_side):
    first, gx, half = is_first(), lax.axis_index("gx"), lax.axis_size("gx") // 2
    target = jnp.where(first, wrap[...], inverse[...])
    column = iota(target.shape, 0) * NJ + iota(target.shape, 1)
    target = jnp.where((gx == half) | (gx == half - 1), column, target)
    upper = lax.rem(lax.axis_index("gy") + 32 - LEAD, 32) >= NZ
    x = rows[pl.ds(jnp.where(first, 0, 32), 32)]
    x = jnp.concatenate([x[32 - LEAD:], x[:32 - LEAD]], 0)
    lane, sub = iota(x.shape, 2), iota(x.shape, 1)

    def after(y):
        return jnp.concatenate([y[1:], y[:1]], 0)

    def before(y):
        return jnp.concatenate([y[-1:], y[:-1]], 0)

    left, right = pltpu.roll(x, NJ - 1, 2), pltpu.roll(x, 1, 2)
    north = jnp.where(lane == NJ - 1, after(left), left)
    south = jnp.where(lane == 0, before(right), right)
    v = jnp.where(upper, x[:, 2:3, :], x[:, 1:2, :])
    k_cell, k_north, k_south = x[:, 3:4, :], north[:, 3:4, :], south[:, 3:4, :]
    term = 0.5 * (
        (k_cell + k_north) * (north - x) + (k_cell + k_south) * (south - x) - v * (north - south)
    )
    x = x + jnp.where((sub >= 4) & (sub < 7), pltpu.roll(term, 4, 1), 0.0)

    part_a = x.astype(jnp.bfloat16).astype(jnp.float32)
    rest = x - part_a
    part_b = rest.astype(jnp.bfloat16).astype(jnp.float32)
    part_c = rest - part_b
    for s in range(32):
        t = target[s:s + 1, :]
        hi, lo = lax.shift_right_logical(t, 8), lax.bitwise_and(t, 255)
        stack = jnp.concatenate([part_a[s], part_b[s], part_c[s]], 0)
        masked = jnp.concatenate([jnp.where(hi == h, stack, 0.0) for h in range(16)], 0)
        at = slice(s * NJ, (s + 1) * NJ)
        left_side[:, at] = masked.astype(jnp.bfloat16)
        right_side[:, at] = jnp.where(iota((256, NJ), 0) == lo, 1.0, 0.0).astype(jnp.bfloat16)
    moved = lax.dot_general(
        left_side[...], right_side[...], (((1,), (1,)), ((), ())), preferred_element_type=jnp.float32
    )
    for h in range(16):
        at = h * 24
        tile = moved[at:at + 8, :] + moved[at + 8:at + 16, :] + moved[at + 16:at + 24, :]
        out[2 * h] = tile[:, 0:NJ]
        out[2 * h + 1] = tile[:, NJ:2 * NJ]
    y = out[...]
    prior, later = before(y), after(y)
    last = jnp.zeros_like(y)
    for r in range(4):
        corner = jnp.where(lane < 64, pltpu.roll(later, r, 2), pltpu.roll(prior, (NJ - r) % NJ, 2))
        corner = pltpu.roll(corner, 7 - r, 1)
        last = jnp.where((lane == r) | (lane == NJ - 1 - r), corner, last)
    y = jnp.where(sub == 7, last, y)
    out[...] = jnp.concatenate([y[LEAD:], y[:LEAD]], 0)


def beside(m, h):
    lane = iota(m.shape, 1)
    m_left, h_left = pltpu.roll(m, NJ - 1, 1), pltpu.roll(h, NJ - 1, 1)
    m_right, h_right = pltpu.roll(m, 1, 1), pltpu.roll(h, 1, 1)
    at_end, at_start = lane == NJ - 1, lane == 0
    return (
        jnp.where(at_end, h_left, m_left),
        jnp.where(at_start, h_right, m_right),
        jnp.where(at_end, m_left, h_left),
        jnp.where(at_start, m_right, h_right),
    )


def rates_of(cells, k_cell, k_sides, drag, sign=None):
    u, v, w = cells[0][0], cells[1][0], cells[2][0]
    resist = drag * jnp.sqrt(u * u + v * v + w * w + SPEED_EPS)
    if sign is not None:
        u = sign * u
    sums = [k_cell + side for side in k_sides]
    total = sums[0] + sums[1] + sums[2] + sums[3] + sums[4] + sums[5]
    rates = []
    for m in range(NF):
        f, e, ws, n, s, up, dn = cells[m]
        rate = 0.5 * (
            (sums[0] - u) * e + (sums[1] + u) * ws
            + (sums[2] - v) * n + (sums[3] + v) * s
            + (sums[4] - w) * up + (sums[5] + w) * dn
            - total * f
        )
        if m < 3:
            rate = rate - resist * f
        if m == 2:
            rate = rate + BUOYANCY * cells[3][0]
        rates.append(rate)
    return rates


def sections_kernel(fields, diff, heights, halo, out, kept, one, one_halo):
    sub = iota((NI, NJ), 0)

    def along(x):
        return (
            jnp.where(sub == NI - 1, 0.0, pltpu.roll(x, NI - 1, 0)),
            jnp.where(sub == 0, 0.0, pltpu.roll(x, 1, 0)),
        )

    high_main = heights[...].astype(jnp.float32)
    high_halo = halo[HALO - 1]

    def section_one(k, _):
        up, dn = jnp.minimum(k + 1, NZ - 1), jnp.maximum(k - 1, 0)
        has_up = jnp.where(k < NZ - 1, 1.0, 0.0).astype(jnp.float32)
        has_dn = jnp.where(k > 0, 1.0, 0.0).astype(jnp.float32)
        level = k.astype(jnp.float32)
        k_main, k_halo = diff[k], halo[NF * NZ + k]
        n, s, hn, hs = beside(k_main, k_halo)
        k_sides = (*along(k_main), n, s, diff[up], diff[dn])
        kh_sides = (*along(k_halo), hn, hs, halo[NF * NZ + up], halo[NF * NZ + dn])
        cells, halos = [], []
        for m in range(NF):
            f, h = fields[m, k], halo[m * NZ + k]
            n, s, hn, hs = beside(f, h)
            cells.append((f, *along(f), n, s, has_up * fields[m, up], has_dn * fields[m, dn]))
            halos.append((h, *along(h), hn, hs, has_up * halo[m * NZ + up], has_dn * halo[m * NZ + dn]))
        drag = jnp.where(level < high_main, DRAG_COEF, 0.0)
        drag_h = jnp.where(level < high_halo, DRAG_COEF, 0.0)
        rates = rates_of(cells, k_main, k_sides, drag)
        rates_h = rates_of(halos, k_halo, kh_sides, drag_h)
        for m in range(NF):
            one[m, k] = cells[m][0] + TIME_STEP / 3.0 * rates[m]
            one_halo[m, k] = halos[m][0] + TIME_STEP / 3.0 * rates_h[m]
        return 0

    lax.fori_loop(0, NZ, section_one, 0, unroll=4)

    def section_two(k, _):
        up, dn = jnp.minimum(k + 1, NZ - 1), jnp.maximum(k - 1, 0)
        has_up = jnp.where(k < NZ - 1, 1.0, 0.0).astype(jnp.float32)
        has_dn = jnp.where(k > 0, 1.0, 0.0).astype(jnp.float32)
        k_main = diff[k]
        n, s, _, _ = beside(k_main, halo[NF * NZ + k])
        k_sides = (*along(k_main), n, s, diff[up], diff[dn])
        cells = []
        for m in range(NF):
            f = one[m, k]
            n, s, _, _ = beside(f, one_halo[m, k])
            cells.append((f, *along(f), n, s, has_up * one[m, up], has_dn * one[m, dn]))
        drag = jnp.where(k.astype(jnp.float32) < high_main, DRAG_COEF, 0.0)
        rates = rates_of(cells, k_main, k_sides, drag)
        for m in range(NF):
            out[m, k] = fields[m, k] + TIME_STEP / 2.0 * rates[m]
        return 0

    lax.fori_loop(0, NZ, section_two, 0, unroll=4)
    for m in range(NF):
        for r in range(3):
            kept[0, m, r] = one[m, :, r, :]
            kept[1, m, r] = one[m, :, NI - 1 - r, :]
        for r in range(2):
            kept[0, m, 3 + r] = one_halo[m, :, r, :]
            kept[1, m, 3 + r] = one_halo[m, :, NI - 1 - r, :]


def redo_side(side, outer, corner, rates, fields, diff, heights, halo, kept, out):
    sign = 1.0 if side == 0 else -1.0
    rows = [r if side == 0 else NI - 1 - r for r in range(3)]

    def block_row(i, r):
        return (diff if i == NF else fields.at[i])[:, rows[r], :]

    def halo_row(i, r):
        return halo[i * NZ:(i + 1) * NZ, rows[r], :]

    own = [block_row(i, 0) for i in range(NA)]
    beyond = [halo_row(i, 0) for i in range(NA)]
    ones, one_halos = [], []
    for m in range(NF):
        rate = rates[m] + 0.5 * (
            (outer[NF] + own[NF]) * (own[m] - outer[m]) - sign * outer[0] * own[m]
        )
        one_out = outer[m] + TIME_STEP / 3.0 * rate
        rate = (own[NF] + outer[NF] + sign * own[0]) * outer[m] - outer[NF] * own[m]
        one_own = kept[side, m, 0] + TIME_STEP / 6.0 * rate
        rate = (beyond[NF] + corner[NF] + sign * beyond[0]) * corner[m] - corner[NF] * beyond[m]
        ones.append([one_out, one_own, kept[side, m, 1], kept[side, m, 2]])
        one_halos.append([kept[side, m, 3] + TIME_STEP / 6.0 * rate, kept[side, m, 4]])
    k_rows = [outer[NF], own[NF], block_row(NF, 1), block_row(NF, 2)]
    k_halos = [beyond[NF], halo_row(NF, 1)]
    for r in range(2):
        k_cell = k_rows[r + 1]
        k_n, k_s, _, _ = beside(k_cell, k_halos[r])
        k_sides = (k_rows[r + 2], k_rows[r], k_n, k_s, *levels(k_cell, True))
        cells = []
        for m in range(NF):
            f = ones[m][r + 1]
            n, s, _, _ = beside(f, one_halos[m][r])
            cells.append((f, ones[m][r + 2], ones[m][r], n, s, *levels(f, False)))
        drag = jnp.where(iota((NZ, NJ), 0) < heights[rows[r]:rows[r] + 1, :], DRAG_COEF, 0.0)
        rates = rates_of(cells, k_cell, k_sides, drag, sign)
        for m in range(NF):
            out[m, :, rows[r], :] = block_row(m, r) + TIME_STEP / 2.0 * rates[m]


def edges_kernel(fields, diff, heights, halo, kept, west, east, done, out):
    out[...] = done[...]
    for side, rim, beyond_wrap, sign in ((0, west, is_first(), 1.0), (1, east, is_last(), -1.0)):
        @pl.when(jnp.logical_not(beyond_wrap))
        def _(side=side, rim=rim, sign=sign):
            outer, far, height = split_rim(rim)
            rates = row_rates(outer, far, height, sign)
            corner = spread_out(rim[EDGE_ROWS:MESSAGE, :])
            corner = [corner[i * NZ:(i + 1) * NZ, :] for i in range(NA)]
            sides = [beside(outer[i], corner[i]) for i in range(NA)]
            k_cell, k_n, k_s = outer[NF], sides[NF][0], sides[NF][1]
            for m in range(NF):
                f, n, s = outer[m], sides[m][0], sides[m][1]
                rates[m] = rates[m] + 0.5 * (
                    (k_cell + k_n) * (n - f) + (k_cell + k_s) * (s - f) - outer[1] * (n - s)
                )
            redo_side(side, outer, corner, rates, fields, diff, heights, halo, kept, out)


def wrap_kernel(fields, diff, heights, halo, kept, wrapped, done, out):
    out[...] = done[...]
    lane = iota((NZ, NJ), 1)
    place = {0: (0, 0), 1: (0, 1), 2: (0, 2), NF: (0, 3), 3: (NZ, 0), 4: (NZ, 1)}
    for side, mine in ((0, is_first()), (1, is_last())):
        @pl.when(mine)
        def _(side=side):
            rates, outer, corner = [], [], []
            for m in range(NF):
                half, row = (0, 4 + m) if m < 3 else (NZ, 1 + m)
                rates.append(wrapped[half:half + NZ, row, :])
            for i in range(NA):
                half, row = place[i]
                outer.append(wrapped[half:half + NZ, row, :])
                spare = wrapped[half:half + NZ, 7, :]
                corner.append(
                    jnp.where(lane < 64, pltpu.roll(spare, (NJ - row) % NJ, 1), pltpu.roll(spare, row, 1))
                )
            redo_side(side, outer, corner, rates, fields, diff, heights, halo, kept, out)


def shards(fields, diffusivity, heights, wrap_map):
    count_x, count_y = lax.axis_size("gx"), lax.axis_size("gy")
    last = count_x - 1
    pack = f32(2, PACK)
    block = (fields, diffusivity, heights)
    half = pltpu.VMEM((NF, NZ, 8, NJ), jnp.float32), pltpu.VMEM((NZ, 8, NJ), jnp.float32)
    packets = pl.pallas_call(
        packet_kernel,
        out_shape=f32(2 * count_y, 8, NJ),
        in_specs=[pl.BlockSpec(memory_space=pl.ANY)] * 3,
        out_specs=VMEM,
        scratch_shapes=[*half, pltpu.VMEM((8, NJ), jnp.int32), pltpu.SemaphoreType.DMA((3,))],
        compiler_params=pltpu.CompilerParams(vmem_limit_bytes=56 * 1024 * 1024),
        name="packets",
    )(*block)

    half_x = count_x // 2
    row_pairs = [(0, last), (half_x, half_x - 1)] + [(i, i + half_x) for i in range(1, half_x - 1)]
    def line(lead, *rows):
        return [r * count_y + (i + lead) % count_y for r in rows for i in range(count_y)]

    groups = [line(LEAD, b, a) for a, b in row_pairs]
    rows = lax.all_to_all(packets, ("gx", "gy"), 0, 0, axis_index_groups=groups)

    low = [(i, i + 1) for i in range(0, count_y, 2)]
    high = [(i, (i + 1) % count_y) for i in range(1, count_y, 2)]
    tied = lax.optimization_barrier((*block, packets))[:3]
    to_a, to_b = call(pack_kernel, (pack, pack), *tied, name="pack")
    from_b = lax.ppermute(to_b, "gy", high + [(j, i) for i, j in high])
    from_a = lax.ppermute(to_a, "gy", low + [(j, i) for i, j in low])

    wrap = wrap_map.reshape(count_y, NJ)
    inverse = call(
        inverse_kernel, jax.ShapeDtypeStruct((count_y, NJ), jnp.int32), wrap, name="inverse"
    )
    rows, inverse, from_a = lax.optimization_barrier((rows, inverse, from_a))
    moved = call(
        permute_kernel, f32(count_y, 8, NJ), rows, wrap, inverse, name="permute",
        scratch=[pltpu.VMEM((384, 32 * NJ), jnp.bfloat16), pltpu.VMEM((256, 32 * NJ), jnp.bfloat16)],
    )
    moved, from_b = lax.optimization_barrier((moved, from_b))
    groups = [line(LEAD, r) for r in range(count_x)]
    wrapped = lax.all_to_all(moved, ("gx", "gy"), 0, 0, axis_index_groups=groups)

    message = f32(MESSAGE, NJ)
    halo, to_east, to_west = call(
        unpack_kernel, (f32(HALO, NI, NJ), message, message),
        from_a, from_b, *block, name="unpack",
            )
    east_pairs = [(i, i + 1) for i in range(last) if i + 1 != half_x]
    west = lax.ppermute(to_east, "gx", east_pairs)
    east = lax.ppermute(to_west, "gx", [(j, i) for i, j in east_pairs])

    state = pltpu.VMEM((NF, NZ, NI, NJ), jnp.float32)
    done, kept = call(
        sections_kernel, (f32(NF, NZ, NI, NJ), f32(2, NF, 5, NZ, NJ)),
        *block, halo, name="sections", scratch=[state, state],
    )
    done = call(
        wrap_kernel, f32(NF, NZ, NI, NJ), *block, halo, kept, wrapped, done, name="wrapped_rows"
    )
    return call(
        edges_kernel, f32(NF, NZ, NI, NJ), *block, halo, kept, west, east, done, name="edges"
    )


def solution(mesh):
    in_specs = (P(None, None, "gx", "gy"), P(None, "gx", "gy"), P("gx", "gy"), P())
    out_specs = P(None, None, "gx", "gy")
    return jax.shard_map(shards, mesh=mesh, in_specs=in_specs, out_specs=out_specs, check_vma=False)
```
